32 devices in a mesh: design: 2 (over x), gx: 16 (over z, y, core).
Axes of the slice: x: 2, y: 2, z: 4, core: 2. Of those that a mesh axis runs over, the one named last changes fastest.
Arguments:
- electric: float32 [3, 128, 128, 128], P(None, ('design', 'gx')), parts along dimension 1, may hold values from -6 to 6
- magnetic: float32 [3, 128, 128, 128], P(None, ('design', 'gx')), parts along dimension 1, may hold values from -6 to 6
- inv_eps: float32 [128, 128, 128], P(('design', 'gx')), parts along dimension 0, may hold values from 0.08 to 1
- accum: float32 [6, 128, 128, 128], P(None, ('design', 'gx')), parts along dimension 1, may hold values from -6 to 6
- forward: float32 [6, 32, 128, 128], P(None, None, ('design', 'gx')), parts along dimension 2, may hold values from -6 to 6
- pillar_ids: int32 [64, 128], P('gx'), may hold values from 0 to 2047, as said below
Outputs:
- electric_out: float32 [3, 128, 128, 128], P(None, ('design', 'gx')), parts along dimension 1
- magnetic_out: float32 [3, 128, 128, 128], P(None, ('design', 'gx')), parts along dimension 1
- accum_out: float32 [6, 128, 128, 128], P(None, ('design', 'gx')), parts along dimension 1
- pillar_grad: float32 [4096], P(('design', 'gx')), parts along dimension 0
The draws below stay inside these ranges and needn't reach their ends.
There are 2 independent parts, one for each index of `design`. The reference program is written for one: setup_inputs(seed, part) draws one part's arguments, and reference() takes and returns one part's arrays. A program takes and returns all parts, laid end to end along the dimension named above; an argument that names none is the same for every part. Nothing has to cross between parts.
Inputs may be any that keep to these rules, and one draw needn't show every extreme that they name: `pillar_ids`: pillars 128 * d to 128 * (d + 1) - 1 are owned by device block d; a column may belong to a pillar of any owner.
All inputs are finite; a program needn't handle non-finite values.
Results may differ from the reference program's by a relative error of at most 0.000076.
Values sent between devices are 32-bit elements; how exact they have to be, the bound alone decides.
No kernel may reach another device: no remote copies, remote signals or barrier semaphores. Data moves between devices by JAX's collectives and lax.ppermute only.
A program may use at most 64 MiB of HBM per device.

```python
import math
import jax
import jax.numpy as jnp
from jax import lax

NY = 128
NZ = 128
DZ = 32
STEPS = 5
ZD0 = 48
NX = 64
PILLARS = 2048


def draw_pillar_ids(key, part):
    key = jax.random.fold_in(key, 7)
    return jax.random.randint(key, (NX, NY), 0, PILLARS).astype(jnp.int32)


def steps_of(own_key, extent, pieces, low, largest):
    loudness = 1.0
    for dim, blocks in pieces:
        steps = jax.random.uniform(jax.random.fold_in(jax.random.fold_in(own_key, 6), dim), (blocks,), jnp.float32, low / len(pieces), largest / len(pieces))
        loudness = loudness * jnp.repeat(jnp.exp(steps), extent[dim] // blocks).reshape((-1,) + (1,) * (len(extent) - 1 - dim))
    return loudness


def centred(rng, dims, spread, most, pieces=(), held_as=jnp.bfloat16):
    values = jax.random.normal(rng, dims, jnp.float32) * spread
    if len(pieces) > 0:
        values = steps_of(rng, dims, pieces, -0.22, 0.18) * values
    return jnp.clip(values, min=-most, max=most).astype(held_as)


def setup_inputs(seed: int = 0, part: int = 0) -> dict:
    key_list = jax.random.split(jax.random.key(seed), 7)
    own_keys = jax.random.split(jax.random.fold_in(key_list[6], part), 7)
    return {
        "electric": centred(own_keys[0], (3, NX, NY, NZ), 1.0, 6.0, ((1, 16),), jnp.float32),
        "magnetic": centred(own_keys[1], (3, NX, NY, NZ), 1.0, 6.0, ((1, 16),), jnp.float32),
        "inv_eps": jnp.clip(jnp.exp(math.log(1.0) - 2.5257287 * jax.random.uniform(own_keys[2], (NX, NY, NZ), jnp.float32) ** steps_of(own_keys[2], (NX, NY, NZ), ((0, 16),), -0.2, 0.2)), 0.08, 1.0),
        "accum": centred(own_keys[3], (6, NX, NY, NZ), 1.0, 6.0, ((1, 16),), jnp.float32),
        "forward": centred(own_keys[4], (6, DZ, NX, NY), 1.0, 6.0, ((2, 16),), jnp.float32),
        "pillar_ids": draw_pillar_ids(jax.random.fold_in(key_list[6], 71), part),
    }


courant = 0.5
angular = 0.3
sens_scale = 0.05


def next_along(field, axis):
    size = field.shape[axis]
    rest = lax.slice_in_dim(field, 1, size, axis=axis)
    return jnp.concatenate([rest, jnp.zeros_like(lax.slice_in_dim(field, 0, 1, axis=axis))], axis)


def prev_along(field, axis):
    size = field.shape[axis]
    rest = lax.slice_in_dim(field, 0, size - 1, axis=axis)
    return jnp.concatenate([jnp.zeros_like(lax.slice_in_dim(field, 0, 1, axis=axis)), rest], axis)


def reference(electric, magnetic, inv_eps, accum, forward, pillar_ids):
    for instant in range(STEPS):
        elec_x, elec_y, elec_z = electric[0], electric[1], electric[2]
        curl_x = next_along(elec_z, 1) - elec_z - (next_along(elec_y, 2) - elec_y)
        curl_y = next_along(elec_x, 2) - elec_x - (next_along(elec_z, 0) - elec_z)
        curl_z = next_along(elec_y, 0) - elec_y - (next_along(elec_x, 1) - elec_x)
        magnetic = magnetic - courant * jnp.stack([curl_x, curl_y, curl_z])
        mag_x, mag_y, mag_z = magnetic[0], magnetic[1], magnetic[2]
        rot_x = mag_z - prev_along(mag_z, 1) - (mag_y - prev_along(mag_y, 2))
        rot_y = mag_x - prev_along(mag_x, 2) - (mag_z - prev_along(mag_z, 0))
        rot_z = mag_y - prev_along(mag_y, 0) - (mag_x - prev_along(mag_x, 1))
        electric = electric + courant * inv_eps[None] * jnp.stack([rot_x, rot_y, rot_z])
        phase = angular * (instant + 1)
        accum = accum + jnp.concatenate([math.cos(phase) * electric, math.sin(phase) * electric])
    slab = accum[:, :, :, ZD0:ZD0 + DZ]
    real_part = jnp.einsum("cxyz,czxy->xy", slab[0:3], forward[0:3], precision=lax.Precision.HIGHEST)
    imag_part = jnp.einsum("cxyz,czxy->xy", slab[3:6], forward[3:6], precision=lax.Precision.HIGHEST)
    sens = sens_scale * (real_part - imag_part)
    pillar_grad = jax.ops.segment_sum(sens.reshape(-1), pillar_ids.reshape(-1), num_segments=PILLARS)
    return electric, magnetic, accum, pillar_grad
```

```python
import functools
import math

import jax
import jax.numpy as jnp
from jax import lax
from jax.experimental import pallas as pl
from jax.experimental.pallas import tpu as pltpu
from jax.sharding import PartitionSpec as P

STEPS = 5
COURANT = 0.5
ANGULAR = 0.3
SENS_SCALE = 0.05
X, Y, Z = 0, 1, 2
VMEM = pl.BlockSpec(memory_space=pltpu.VMEM)
SMEM = pl.BlockSpec(memory_space=pltpu.SMEM)


def shifted(field, axis, ahead):
    size = field.shape[axis]
    where = lax.broadcasted_iota(jnp.int32, field.shape, axis)
    if ahead:
        return jnp.where(where == size - 1, 0.0, pltpu.roll(field, size - 1, axis))
    return jnp.where(where == 0, 0.0, pltpu.roll(field, 1, axis))


def magnetic_plane(elec, beyond, mag):
    ex, ey, ez = elec
    curl_x = shifted(ez, 0, True) - ez - (shifted(ey, 1, True) - ey)
    far_y, far_z = beyond if beyond is not None else (0.0, 0.0)
    curl_y = shifted(ex, 1, True) - ex - (far_z - ez)
    curl_z = far_y - ey - (shifted(ex, 0, True) - ex)
    return [
        None if m is None else m - COURANT * c
        for m, c in zip(mag, (curl_x, curl_y, curl_z))
    ]


def electric_plane(mag, before, elec, eps):
    hx, hy, hz = mag
    past_y, past_z = before if before is not None else (0.0, 0.0)
    rot_x = hz - shifted(hz, 0, False) - (hy - shifted(hy, 1, False))
    rot_y = hx - shifted(hx, 1, False) - (hz - past_z)
    rot_z = hy - past_y - (hx - shifted(hx, 0, False))
    half = COURANT * eps
    return [e + half * r for e, r in zip(elec, (rot_x, rot_y, rot_z))]


def planes(ref, p):
    return [ref[c, p] for c in range(3)]


def store(ref, p, values):
    for c, v in enumerate(values):
        ref[c, p] = v


def magnetic_all(elec, mag, count, beyond):
    for p in range(count):
        far = (elec[Y, p + 1], elec[Z, p + 1]) if p + 1 < count else beyond
        store(mag, p, magnetic_plane(planes(elec, p), far, planes(mag, p)))


def electric_all(elec, mag, eps, count, before):
    for p in range(count):
        past = (mag[Y, p - 1], mag[Z, p - 1]) if p else before
        store(elec, p, electric_plane(planes(mag, p), past, planes(elec, p), eps[p]))


def opening_kernel(role, elec, mag, eps, far_msg, near_msg):
    last = elec.shape[1] - 1
    even = role[0] == 0
    mid = magnetic_plane(planes(elec, last), None, (None, mag[Y, last], mag[Z, last]))
    mine = (elec[Y, 0], elec[Z, 0])

    @pl.when(even)
    def _():
        for k in range(2):
            near_msg[k] = mid[1 + k]
            far_msg[k] = mine[k]
            far_msg[2 + k] = eps[k]

    @pl.when(jnp.logical_not(even))
    def _():
        for k in range(2):
            near_msg[k] = mine[k]
            far_msg[k] = mid[1 + k]
            far_msg[2 + k] = eps[last - k]


def closed_kernel(role, elec_in, mag_in, eps, near, *rest):
    outs, (elec, mag) = rest[:-2], rest[-2:]
    count = elec_in.shape[1]
    last = count - 1
    even = role[0] == 0

    def send(step, k, value):
        ref = outs[(step - 2) // 2]
        ref[(step % 2) * 2 + k] = value

    @pl.when(even)
    def _():
        src_e, src_m = elec_in, mag_in
        for step in range(1, STEPS):
            keep = min(count, STEPS - step)
            for p in range(keep):
                if p + 1 < count:
                    far = (src_e[Y, p + 1], src_e[Z, p + 1])
                else:
                    far = (near[0], near[1])
                store(mag, p, magnetic_plane(planes(src_e, p), far, planes(src_m, p)))
            for p in range(keep):
                past = (mag[Y, p - 1], mag[Z, p - 1]) if p else None
                new = electric_plane(planes(mag, p), past, planes(src_e, p), eps[p])
                store(elec, p, new)
                if p == 0:
                    send(step + 1, 0, new[Y])
                    send(step + 1, 1, new[Z])
            src_e, src_m = elec, mag

    @pl.when(jnp.logical_not(even))
    def _():
        src_e, src_m = elec_in, mag_in
        for step in range(1, STEPS + 1):
            low = max(0, count - (STEPS + 1 - step))
            for p in range(low, count):
                far = (src_e[Y, p + 1], src_e[Z, p + 1]) if p < last else None
                new = magnetic_plane(planes(src_e, p), far, planes(src_m, p))
                store(mag, p, new)
                if p == last and step > 1:
                    send(step, 0, new[Y])
                    send(step, 1, new[Z])
            if step == STEPS:
                break
            low = max(0, count - (STEPS - step))
            for p in range(low, count):
                if p:
                    past = (mag[Y, p - 1], mag[Z, p - 1])
                else:
                    past = (
                        near[0] + COURANT * src_e[Z, 0],
                        near[1] - COURANT * src_e[Y, 0],
                    )
                store(elec, p, electric_plane(planes(mag, p), past, planes(src_e, p), eps[p]))
            src_e, src_m = elec, mag


LEFT_MAG = {1: 1, 2: 2, 3: 3, 4: 2, 5: 1}
LEFT_ELEC = {1: 1, 2: 2, 3: 2, 4: 1, 5: 0}
RIGHT_MAG = {1: 0, 2: 1, 3: 2, 4: 1, 5: 0}
RIGHT_ELEC = {1: 1, 2: 2, 3: 2, 4: 1, 5: 0}


def beyond_left(step, elec, side_e, side_m):
    for j in range(LEFT_MAG[step]):
        if j == 0:
            far = (elec[Y, 0], elec[Z, 0])
        else:
            far = (side_e[Y, j - 1], side_e[Z, j - 1])
        new = magnetic_plane(planes(side_e, j), far, planes(side_m, j))
        store(side_m, j, new)


def beyond_left_electric(step, side_e, side_m, side_eps):
    for j in range(LEFT_ELEC[step]):
        past = (side_m[Y, j + 1], side_m[Z, j + 1])
        store(side_e, j, electric_plane(planes(side_m, j), past, planes(side_e, j), side_eps[j]))


def beyond_right(step, mag, side_e, side_m, side_eps, last):
    for j in range(RIGHT_MAG[step]):
        far = (side_e[Y, j + 1], side_e[Z, j + 1])
        store(side_m, j, magnetic_plane(planes(side_e, j), far, planes(side_m, j)))
    for j in range(RIGHT_ELEC[step]):
        if j == 0:
            past = (mag[Y, last], mag[Z, last])
        else:
            past = (side_m[Y, j - 1], side_m[Z, j - 1])
        store(side_e, j, electric_plane(planes(side_m, j), past, planes(side_e, j), side_eps[j]))


def open_kernel(step, *refs):
    names = ["role", "elec_in", "mag_in", "eps", "accum_in", "near", "far", "opening"]
    if step > 1:
        names += ["side_e_in", "side_m_in"]
    if step == STEPS:
        names += ["weights", "high", "low"]
    names += ["elec", "mag", "accum"]
    names += ["next_msg", "side_e", "side_m"] if step < STEPS else ["pillars", "side_e", "side_m"]
    r = dict(zip(names, refs, strict=True))
    role, near, far, eps = r["role"], r["near"], r["far"], r["eps"]
    elec_in, mag_in, elec, mag = r["elec_in"], r["mag_in"], r["elec"], r["mag"]
    side_e, side_m = r["side_e"], r["side_m"]
    side_eps = r["opening"].at[2:4]
    count = elec.shape[1]
    last = count - 1
    even = role[0] == 0
    at = 0 if step == 1 else (step % 2) * 2
    if step == 1:
        side_e[...] = jnp.zeros_like(side_e)
        side_m[...] = jnp.zeros_like(side_m)
    else:
        side_e[...] = r["side_e_in"][...]
        side_m[...] = r["side_m_in"][...]

    scale_far = jnp.where(even, role[1], role[2]).astype(jnp.float32)

    def run(is_even):
        if is_even:
            beyond = (near[0], near[1])
            beyond_left(step, elec_in, side_e, side_m)
            past0 = (
                (far[at] + side_m[Y, 0]) * scale_far,
                (far[at + 1] + side_m[Z, 0]) * scale_far,
            )
        else:
            beyond = (
                (far[at] + side_e[Y, 0]) * scale_far,
                (far[at + 1] + side_e[Z, 0]) * scale_far,
            )
            past0 = (
                near[0] + COURANT * elec_in[Z, 0],
                near[1] - COURANT * elec_in[Y, 0],
            )
        for p in range(count):
            nxt = (elec_in[Y, p + 1], elec_in[Z, p + 1]) if p < last else beyond
            store(mag, p, magnetic_plane(planes(elec_in, p), nxt, planes(mag_in, p)))
        if is_even:
            beyond_left_electric(step, side_e, side_m, side_eps)
        else:
            beyond_right(step, mag, side_e, side_m, side_eps, last)
        phase = ANGULAR * step
        for p in range(count):
            past = (mag[Y, p - 1], mag[Z, p - 1]) if p else past0
            new = electric_plane(planes(mag, p), past, planes(elec_in, p), eps[p])
            store(elec, p, new)
            total = None
            for c in range(3):
                for part, wave in ((0, math.cos(phase)), (3, math.sin(phase))):
                    value = r["accum_in"][part + c, p] + wave * new[c]
                    r["accum"][part + c, p] = value
                    if step == STEPS:
                        term = value * r["weights"][part + c, p]
                        total = term if total is None else total + term
            if step == STEPS:
                yield p, total
        if step < STEPS:
            if is_even:
                mid = magnetic_plane(
                    planes(elec, last), None, (None, mag[Y, last], mag[Z, last])
                )
                r["next_msg"][0] = mid[1]
                r["next_msg"][1] = mid[2]
            else:
                r["next_msg"][0] = elec[Y, 0]
                r["next_msg"][1] = elec[Z, 0]

    def whole(is_even):
        sums = None
        for p, total in run(is_even):
            row = lax.dot_general(
                jnp.ones((8, total.shape[1]), jnp.float32), total, (((1,), (1,)), ((), ())),
                precision=lax.Precision.HIGHEST, preferred_element_type=jnp.float32,
            )[0:1]
            owners = r["pillars"].shape[0]
            label = lax.broadcasted_iota(jnp.int32, (owners, total.shape[0]), 0)
            spread = jnp.where(label == r["high"][p : p + 1], row, 0.0)
            term = lax.dot_general(
                spread, r["low"][p], (((1,), (0,)), ((), ())),
                precision=lax.Precision.HIGHEST, preferred_element_type=jnp.float32,
            )
            sums = term if sums is None else sums + term
        if sums is not None:
            r["pillars"][...] = sums

    pl.when(even)(functools.partial(whole, True))
    pl.when(jnp.logical_not(even))(functools.partial(whole, False))


def call(kernel, args, outs, scratch=(), aliases=None, flops=10**6):
    return pl.pallas_call(
        kernel,
        out_shape=outs,
        in_specs=[SMEM] + [VMEM] * (len(args) - 1),
        out_specs=[VMEM] * len(outs),
        scratch_shapes=scratch,
        input_output_aliases=aliases or {},
        compiler_params=pltpu.CompilerParams(vmem_limit_bytes=40 * 2**20),
        cost_estimate=pl.CostEstimate(flops=flops, bytes_accessed=10**6, transcendentals=0),
    )(*args)


def shape_of(*dims):
    return jax.ShapeDtypeStruct(dims, jnp.float32)


def halved(sums, axis):
    size = lax.axis_size(axis)
    me = lax.axis_index(axis)
    bits = size.bit_length() - 1
    block = sums
    for bit in range(bits):
        pair = block.reshape(-1, 2, block.shape[-1])
        mine = (me >> bit) & 1
        keep = jnp.where(mine == 0, pair[:, 0], pair[:, 1])
        give = jnp.where(mine == 0, pair[:, 1], pair[:, 0])
        block = keep + lax.ppermute(give, axis, [(i, i ^ (1 << bit)) for i in range(size)])
    return block.reshape(-1)


def per_device(electric, magnetic, inv_eps, accum, forward, pillar_ids):
    size = lax.axis_size("gx")
    me = lax.axis_index("gx")
    role = jnp.stack([me % 2, jnp.where(me == 0, 0, 1), jnp.where(me == size - 1, 0, 1)]).astype(jnp.int32)
    count, ny, nz = inv_eps.shape
    same_chip = [(i, i ^ 1) for i in range(size)]
    inner = range(1, size - 1, 2)
    next_chip = [(i, i + 1) for i in inner] + [(i + 1, i) for i in inner]

    depth = forward.shape[1]
    start_z = (nz - depth) // 2
    signs = SENS_SCALE * jnp.array([1, 1, 1, -1, -1, -1], jnp.float32)[:, None, None, None]
    weights = jnp.pad(
        signs * jnp.transpose(forward, (0, 2, 3, 1)),
        ((0, 0), (0, 0), (0, 0), (start_z, nz - depth - start_z)),
    )
    per_owner = ny
    high = pillar_ids // per_owner
    low = (pillar_ids % per_owner)[:, :, None] == jnp.arange(per_owner, dtype=jnp.int32)
    low = low.astype(jnp.float32)

    opening, near = call(
        opening_kernel, [role, electric, magnetic, inv_eps], [shape_of(4, ny, nz), shape_of(2, ny, nz)]
    )
    far0 = lax.ppermute(opening, "gx", next_chip)
    near = lax.ppermute(near, "gx", same_chip)
    later = call(
        closed_kernel,
        [role, electric, magnetic, inv_eps, near],
        [shape_of(4, ny, nz), shape_of(4, ny, nz)],
        scratch=[pltpu.VMEM(electric.shape, jnp.float32)] * 2,
    )
    fars = [lax.ppermute(m, "gx", next_chip) for m in later]

    field = shape_of(*electric.shape)
    side = shape_of(3, 3, ny, nz)
    sides = []
    for step in range(1, STEPS + 1):
        far = far0 if step == 1 else fars[(step - 2) // 2]
        args = [role, electric, magnetic, inv_eps, accum, near, far, far0] + sides
        if step < STEPS:
            outs = [field, field, shape_of(*accum.shape), shape_of(2, ny, nz), side, side]
            aliases = {} if step == 1 else {1: 0, 2: 1, 4: 2, 8: 4, 9: 5}
            electric, magnetic, accum, near, *sides = call(
                functools.partial(open_kernel, step), args, outs, aliases=aliases
            )
            near = lax.ppermute(near, "gx", same_chip)
        else:
            args += [weights, high, low]
            outs = [field, field, shape_of(*accum.shape), shape_of(size, per_owner)]
            scratch = [pltpu.VMEM(side.shape, jnp.float32)] * 2
            electric, magnetic, accum, sums = call(
                functools.partial(open_kernel, step), args, outs, scratch=scratch
            )
    return electric, magnetic, accum, halved(sums, "gx")


def solution(mesh):
    return jax.shard_map(
        per_device,
        mesh=mesh,
        in_specs=(
            P(None, ("design", "gx"), None, None),
            P(None, ("design", "gx"), None, None),
            P(("design", "gx"), None, None),
            P(None, ("design", "gx"), None, None),
            P(None, None, ("design", "gx"), None),
            P("gx", None),
        ),
        out_specs=(
            P(None, ("design", "gx"), None, None),
            P(None, ("design", "gx"), None, None),
            P(None, ("design", "gx"), None, None),
            P(("design", "gx")),
        ),
        check_vma=False,
    )
```

```python
import functools
import math

import jax
import jax.numpy as jnp
from jax import lax
from jax.experimental import pallas as pl
from jax.experimental.pallas import tpu as pltpu
from jax.sharding import PartitionSpec as P

STEPS = 5
COURANT = 0.5
ANGULAR = 0.3
SENS_SCALE = 0.05
X, Y, Z = 0, 1, 2
VMEM = pl.BlockSpec(memory_space=pltpu.VMEM)
SMEM = pl.BlockSpec(memory_space=pltpu.SMEM)


def shifted(field, axis, ahead):
    size = field.shape[axis]
    where = lax.broadcasted_iota(jnp.int32, field.shape, axis)
    if ahead:
        return jnp.where(where == size - 1, 0.0, pltpu.roll(field, size - 1, axis))
    return jnp.where(where == 0, 0.0, pltpu.roll(field, 1, axis))


def magnetic_plane(elec, beyond, mag):
    ex, ey, ez = elec
    curl_x = shifted(ez, 0, True) - ez - (shifted(ey, 1, True) - ey)
    far_y, far_z = beyond if beyond is not None else (0.0, 0.0)
    curl_y = shifted(ex, 1, True) - ex - (far_z - ez)
    curl_z = far_y - ey - (shifted(ex, 0, True) - ex)
    return [
        None if m is None else m - COURANT * c
        for m, c in zip(mag, (curl_x, curl_y, curl_z))
    ]


def electric_plane(mag, before, elec, eps):
    hx, hy, hz = mag
    past_y, past_z = before if before is not None else (0.0, 0.0)
    rot_x = hz - shifted(hz, 0, False) - (hy - shifted(hy, 1, False))
    rot_y = hx - shifted(hx, 1, False) - (hz - past_z)
    rot_z = hy - past_y - (hx - shifted(hx, 0, False))
    half = COURANT * eps
    return [e + half * r for e, r in zip(elec, (rot_x, rot_y, rot_z))]


def planes(ref, p):
    return [ref[c, p] for c in range(3)]


def store(ref, p, values):
    for c, v in enumerate(values):
        ref[c, p] = v


def magnetic_all(elec, mag, count, beyond):
    for p in range(count):
        far = (elec[Y, p + 1], elec[Z, p + 1]) if p + 1 < count else beyond
        store(mag, p, magnetic_plane(planes(elec, p), far, planes(mag, p)))


def electric_all(elec, mag, eps, count, before):
    for p in range(count):
        past = (mag[Y, p - 1], mag[Z, p - 1]) if p else before
        store(elec, p, electric_plane(planes(mag, p), past, planes(elec, p), eps[p]))


WINDOW = 42
LOW = 43


def turned(plane, by):
    return pltpu.roll(plane, by % plane.shape[1], 1)


def packed(a, b, c):
    lane = lax.broadcasted_iota(jnp.int32, a.shape, 1)
    last = jnp.where(lane < LOW + 2 * WINDOW, turned(b, WINDOW), turned(c, WINDOW))
    core = jnp.where(
        lane < LOW, turned(c, -WINDOW), jnp.where(lane < LOW + WINDOW, a, last)
    )
    inside = jnp.logical_and(lane >= LOW, lane < LOW + WINDOW)
    rest_a = jnp.where(inside, turned(c, LOW), a)
    rest_b = jnp.where(inside, turned(c, -LOW), b)
    return core, rest_a, rest_b


def unpacked(core, rests):
    b = turned(core, -WINDOW)
    c = turned(core, WINDOW)
    if rests is None:
        return core, b, c
    rest_a, rest_b = rests
    lane = lax.broadcasted_iota(jnp.int32, core.shape, 1)
    inside = jnp.logical_and(lane >= LOW, lane < LOW + WINDOW)
    end = LOW + WINDOW
    outer = jnp.where(lane == end, b, turned(rest_b, LOW))
    c = jnp.where(lane < LOW - 1, turned(rest_a, -LOW), jnp.where(lane < end, c, outer))
    return jnp.where(inside, core, rest_a), jnp.where(inside, b, rest_b), c


def opening_kernel(role, first_y, first_z, last_e, last_hy, last_hz, eps, msg):
    even = role[0] == 0

    @pl.when(even)
    def _():
        for k, v in enumerate(packed(first_y[0, 0], first_z[0, 0], eps[0])):
            msg[k] = v

    @pl.when(jnp.logical_not(even))
    def _():
        mid = magnetic_plane(planes(last_e, 0), None, (None, last_hy[0, 0], last_hz[0, 0]))[1:]
        for k, v in enumerate(packed(*mid, eps[0])):
            msg[k] = v


def needed(wanted_mag, wanted_elec, count):
    mag, elec = dict(wanted_mag), dict(wanted_elec)
    for step in range(STEPS, 0, -1):
        elec[step] = set(elec.get(step, ()))
        mag[step] = set(mag.get(step, ()))
        mag[step] |= elec[step] | {p - 1 for p in elec[step] if p}
        elec[step - 1] = set(elec.get(step - 1, ())) | elec[step] | mag[step]
        elec[step - 1] |= {p + 1 for p in mag[step] if p + 1 < count}
        mag[step - 1] = set(mag.get(step - 1, ())) | mag[step]
    return mag, elec


def closed_kernel(role, own_e, own_m, own_eps, mate_e, mate_m, mate_eps, core_msg, rest_msg, nears, elec, mag, raw):
    half = own_e.shape[1]
    count = 2 * half
    even = role[0] == 0
    spot = {2: (0, 1), 3: (3, 4), 4: (5, 6), 5: (7, 8)}

    def run(is_even):
        steps = range(1, STEPS + 1)
        if is_even:
            raw[2] = own_eps[1]
            want_m, want_e = {}, {s: {0, half} for s in steps if s < STEPS}
        else:
            raw[2] = own_eps[half - 2]
            want_m, want_e = {s: {half - 1, count - 1} for s in steps}, {}
        need_m, need_e = needed(want_m, want_e, count)

        def first(own, mate, p):
            ref = own if (p < half) == is_even else mate
            return ref, p % half

        def all_of(step, pair, ref, p):
            if step > 1:
                return planes(ref, p)
            return planes(*first(*pair, p))

        def two_of(step, pair, ref, p):
            return tuple(all_of(step, pair, ref, p)[1:])

        pair_e, pair_m = (own_e, mate_e), (own_m, mate_m)
        if is_even:
            for k in range(2):
                nears[k] = mate_e[1 + k, 0]
        for step in steps:
            for p in sorted(need_m[step]):
                far = two_of(step, pair_e, elec, p + 1) if p + 1 < count else None
                here = all_of(step, pair_e, elec, p)
                new = magnetic_plane(here, far, all_of(step, pair_m, mag, p))
                store(mag, p, new)
                if not is_even and p == count - 1 and step > 1:
                    for k in range(2):
                        raw[spot[step][k]] = new[1 + k]
                if not is_even and p == half - 1:
                    nears[2 * (step - 1)] = new[Y] - COURANT * far[1]
                    nears[2 * (step - 1) + 1] = new[Z] + COURANT * far[0]
            for p in sorted(need_e[step]):
                past = (mag[Y, p - 1], mag[Z, p - 1]) if p else None
                ref, at = first(own_eps, mate_eps, p)
                new = electric_plane(planes(mag, p), past, all_of(step, pair_e, elec, p), ref[at])
                store(elec, p, new)
                if is_even and p == 0:
                    for k in range(2):
                        raw[spot[step + 1][k]] = new[1 + k]
                if is_even and p == half:
                    for k in range(2):
                        nears[2 * step + k] = new[1 + k]

    pl.when(even)(functools.partial(run, True))
    pl.when(jnp.logical_not(even))(functools.partial(run, False))
    for g in range(3):
        core, rest_a, rest_b = packed(raw[3 * g], raw[3 * g + 1], raw[3 * g + 2])
        core_msg[g] = core
        rest_msg[2 * g] = rest_a
        rest_msg[2 * g + 1] = rest_b


def past_near(near, elec):
    return (near[0] + COURANT * elec[Z, 0], near[1] - COURANT * elec[Y, 0])


def late_kernel(role, first_y, first_z, eps, opening, msg):
    even = role[0] == 0
    far = unpacked(opening[0], (opening[1], opening[2]))[:2]
    scale = jnp.where(even, role[1], role[2]).astype(jnp.float32)
    for p in range(eps.shape[0]):
        scale = scale * (COURANT * COURANT * eps[p])
    mine = jnp.where(even, COURANT, 0.0)
    msg[0] = scale * (far[0] + mine * first_z[0, 0])
    msg[1] = scale * (far[1] - mine * first_y[0, 0])


def weights_kernel(forward, accum, weights, base):
    depth, count, ny = forward.shape[1:]
    nz = weights.shape[3]
    blank = jnp.zeros(((nz - depth) // 2, ny), jnp.float32)
    for p in range(count):
        total = None
        for c in range(6):
            slab = forward[c, :, p, :] * (SENS_SCALE if c < 3 else -SENS_SCALE)
            w = jnp.transpose(jnp.concatenate([blank, slab, blank], 0))
            weights[c, p] = w
            term = w * accum[c, p]
            total = term if total is None else total + term
        base[p] = total


LEFT_MAG = {1: 1, 2: 2, 3: 3, 4: 2, 5: 1}
LEFT_ELEC = {1: 1, 2: 2, 3: 2, 4: 1, 5: 0}
RIGHT_MAG = {1: 0, 2: 1, 3: 2, 4: 1, 5: 0}
RIGHT_ELEC = {1: 1, 2: 2, 3: 2, 4: 1, 5: 0}


def beyond_left(step, elec, side_e, side_m):
    for j in range(LEFT_MAG[step]):
        if j == 0:
            far = (elec[Y, 0], elec[Z, 0])
        else:
            far = (side_e[Y, j - 1], side_e[Z, j - 1])
        store(side_m, j, magnetic_plane(planes(side_e, j), far, planes(side_m, j)))


def beyond_left_electric(step, side_e, side_m, side_eps):
    for j in range(LEFT_ELEC[step]):
        past = (side_m[Y, j + 1], side_m[Z, j + 1])
        store(side_e, j, electric_plane(planes(side_m, j), past, planes(side_e, j), side_eps[j]))


def beyond_right(step, mag, side_e, side_m, side_eps, last):
    for j in range(RIGHT_MAG[step]):
        far = (side_e[Y, j + 1], side_e[Z, j + 1])
        store(side_m, j, magnetic_plane(planes(side_e, j), far, planes(side_m, j)))
    for j in range(RIGHT_ELEC[step]):
        if j == 0:
            past = (mag[Y, last], mag[Z, last])
        else:
            past = (side_m[Y, j - 1], side_m[Z, j - 1])
        store(side_e, j, electric_plane(planes(side_m, j), past, planes(side_e, j), side_eps[j]))


def open_kernel(slab, role, elec_0, mag_0, eps, nears, late, *refs):
    if slab:
        opening, cores, weights, base, high, low, pillars, elec, mag, side_e, side_m, far = refs
    else:
        opening, cores, others, accum_0, elec, mag, accum, side_e, side_m, far = refs
    count = eps.shape[0]
    last = count - 1
    even = role[0] == 0
    side_e[...] = jnp.zeros_like(side_e)
    side_m[...] = jnp.zeros_like(side_m)
    spots = ((0, 1, 10), (2, 3, 11), (4, 5, 6), (7, 8, 9))
    for g, spot in enumerate(spots):
        if g == 0:
            core, rests = opening[0], (opening[1], opening[2])
        else:
            core = cores[g - 1]
            rests = None if slab else (others[2 * g - 2], others[2 * g - 1])
        for k, v in zip(spot, unpacked(core, rests)):
            far[k] = v
    side_eps = far.at[10:12]

    def run(is_even):
        totals = [base[p] for p in range(count)] if slab else None
        scale = role[1 if is_even else 2].astype(jnp.float32)
        for step in range(1, STEPS + 1):
            src_e, src_m = (elec_0, mag_0) if step == 1 else (elec, mag)
            at = 2 * (step - 1)
            near = (nears[at], nears[at + 1])
            if step == STEPS:
                near = (near[0] + late[0], near[1] + late[1])
            if is_even:
                beyond = near
                beyond_left(step, src_e, side_e, side_m)
                past0 = ((far[at] + side_m[Y, 0]) * scale, (far[at + 1] + side_m[Z, 0]) * scale)
            else:
                beyond = ((far[at] + side_e[Y, 0]) * scale, (far[at + 1] + side_e[Z, 0]) * scale)
                past0 = past_near(near, src_e)
            for p in range(count):
                nxt = (src_e[Y, p + 1], src_e[Z, p + 1]) if p < last else beyond
                store(mag, p, magnetic_plane(planes(src_e, p), nxt, planes(src_m, p)))
            if is_even:
                beyond_left_electric(step, side_e, side_m, side_eps)
            else:
                beyond_right(step, mag, side_e, side_m, side_eps, last)
            waves = (math.cos(ANGULAR * step), math.sin(ANGULAR * step))
            for p in range(count):
                past = (mag[Y, p - 1], mag[Z, p - 1]) if p else past0
                new = electric_plane(planes(mag, p), past, planes(src_e, p), eps[p])
                if not slab or step < STEPS:
                    store(elec, p, new)
                if slab:
                    for c in range(3):
                        mix = waves[0] * weights[c, p] + waves[1] * weights[3 + c, p]
                        totals[p] = totals[p] + mix * new[c]
                    continue
                src_a = accum_0 if step == 1 else accum
                for c in range(6):
                    accum[c, p] = src_a[c, p] + waves[c // 3] * new[c % 3]
        if not slab:
            return
        owners = pillars.shape[0]
        sums = None
        for p, total in enumerate(totals):
            row = lax.dot_general(
                jnp.ones((8, total.shape[1]), jnp.float32), total, (((1,), (1,)), ((), ())),
                precision=lax.Precision.HIGHEST, preferred_element_type=jnp.float32,
            )[0:1]
            label = lax.broadcasted_iota(jnp.int32, (owners, total.shape[0]), 0)
            spread = jnp.where(label == high[p : p + 1], row, 0.0)
            term = lax.dot_general(
                spread, low[p], (((1,), (0,)), ((), ())),
                precision=lax.Precision.HIGHEST, preferred_element_type=jnp.float32,
            )
            sums = term if sums is None else sums + term
        pillars[...] = sums

    pl.when(even)(functools.partial(run, True))
    pl.when(jnp.logical_not(even))(functools.partial(run, False))


def call(kernel, args, outs, scratch=(), smem=1):
    return pl.pallas_call(
        kernel,
        out_shape=[shape_of(*o) for o in outs],
        in_specs=[SMEM] * smem + [VMEM] * (len(args) - smem),
        out_specs=[VMEM] * len(outs),
        scratch_shapes=[pltpu.VMEM(d, jnp.float32) for d in scratch],
        compiler_params=pltpu.CompilerParams(vmem_limit_bytes=24 * 2**20),
        cost_estimate=pl.CostEstimate(flops=1, bytes_accessed=1, transcendentals=0),
    )(*args)


def opening_call(role, elec, mag, eps):
    _, count, ny, nz = elec.shape

    def plane(c, p):
        return pl.BlockSpec((1, 1, ny, nz), lambda i, role: (c, p, 0, 0))

    return pl.pallas_call(
        opening_kernel,
        out_shape=shape_of(3, ny, nz),
        grid_spec=pltpu.PrefetchScalarGridSpec(
            num_scalar_prefetch=1,
            grid=(1,),
            in_specs=[
                plane(Y, 0),
                plane(Z, 0),
                pl.BlockSpec((3, 1, ny, nz), lambda i, role: (0, count - 1, 0, 0)),
                plane(Y, count - 1),
                plane(Z, count - 1),
                pl.BlockSpec((1, ny, nz), lambda i, role: (role[0] * (count - 1), 0, 0)),
            ],
            out_specs=pl.BlockSpec((3, ny, nz), lambda i, role: (0, 0, 0)),
        ),
        compiler_params=pltpu.CompilerParams(vmem_limit_bytes=8 * 2**20),
        cost_estimate=pl.CostEstimate(flops=1, bytes_accessed=1, transcendentals=0),
    )(role, *(pltpu.with_memory_space_constraint(a, pltpu.HBM) for a in (elec, elec, elec, mag, mag, eps)))


def late_call(role, elec, eps, opening):
    _, count, ny, nz = elec.shape

    def plane(c):
        return pl.BlockSpec((1, 1, ny, nz), lambda i, role: (c, 0, 0, 0))

    return pl.pallas_call(
        late_kernel,
        out_shape=shape_of(2, ny, nz),
        grid_spec=pltpu.PrefetchScalarGridSpec(
            num_scalar_prefetch=1,
            grid=(1,),
            in_specs=[
                plane(Y),
                plane(Z),
                pl.BlockSpec((count, ny, nz), lambda i, role: (0, 0, 0)),
                pl.BlockSpec((3, ny, nz), lambda i, role: (0, 0, 0)),
            ],
            out_specs=pl.BlockSpec((2, ny, nz), lambda i, role: (0, 0, 0)),
        ),
        compiler_params=pltpu.CompilerParams(vmem_limit_bytes=8 * 2**20),
        cost_estimate=pl.CostEstimate(flops=1, bytes_accessed=1, transcendentals=0),
    )(role, elec, elec, eps, opening)


def shape_of(*dims):
    return jax.ShapeDtypeStruct(dims, jnp.float32)


def halved(sums, axis):
    size = lax.axis_size(axis)
    me = lax.axis_index(axis)
    bits = size.bit_length() - 1
    block = sums
    for bit in range(bits):
        pair = block.reshape(-1, 2, block.shape[-1])
        mine = (me >> bit) & 1
        keep = jnp.where(mine == 0, pair[:, 0], pair[:, 1])
        give = jnp.where(mine == 0, pair[:, 1], pair[:, 0])
        block = keep + lax.ppermute(give, axis, [(i, i ^ (1 << bit)) for i in range(size)])
    return block.reshape(-1)


def per_device(electric, magnetic, inv_eps, accum, forward, pillar_ids):
    size = lax.axis_size("gx")
    me = lax.axis_index("gx")
    role = jnp.stack([me % 2, jnp.where(me == 0, 0, 1), jnp.where(me == size - 1, 0, 1)]).astype(jnp.int32)
    count, ny, nz = inv_eps.shape
    same_chip = [(i, i ^ 1) for i in range(size)]
    inner = range(1, size - 1, 2)
    next_chip = [(i, i + 1) for i in inner] + [(i + 1, i) for i in inner]

    per_owner = ny
    high = pillar_ids // per_owner
    low = (pillar_ids % per_owner)[:, :, None] == jnp.arange(per_owner, dtype=jnp.int32)
    low = low.astype(jnp.float32)
    field, side = electric.shape, (3, 3, ny, nz)

    def to_mate(block):
        return lax.ppermute(block, "gx", same_chip)

    def to_chip(block):
        return lax.ppermute(block, "gx", next_chip)

    opening = to_chip(opening_call(role, electric, magnetic, inv_eps))
    fixed = [role, electric, magnetic, inv_eps]
    mate = [to_mate(electric), to_mate(magnetic), to_mate(inv_eps)]
    cores, others, nears = call(
        closed_kernel,
        fixed + mate,
        [(3, ny, nz), (6, ny, nz), (2 * STEPS, ny, nz)],
        scratch=[(3, 2 * count, ny, nz)] * 2 + [(9, ny, nz)],
    )
    cores = to_chip(cores)
    opening, nears = lax.optimization_barrier((opening, nears))
    late = to_mate(late_call(role, electric, inv_eps, opening))
    cores, others = lax.optimization_barrier((cores, others))
    others = to_chip(others)
    weights, base = call(weights_kernel, [forward, accum], [accum.shape, inv_eps.shape], smem=0)
    scratch = [side, side, (12, ny, nz)]
    def pillar_sums(args):
        (sums,) = call(
            functools.partial(open_kernel, True),
            args,
            [(size, per_owner)],
            scratch=[field, field] + scratch,
        )
        return halved(sums, "gx")

    grads = lax.cond(
        role[1] < 2,
        pillar_sums,
        lambda args: jnp.zeros((per_owner,), jnp.float32),
        fixed + [nears, late, opening, cores, weights, base, high, low],
    )
    electric, magnetic, accum = call(
        functools.partial(open_kernel, False),
        fixed + [nears, late, opening, cores, others, accum],
        [field, field, accum.shape],
        scratch=scratch,
    )
    return electric, magnetic, accum, grads


def solution(mesh):
    return jax.shard_map(
        per_device,
        mesh=mesh,
        in_specs=(
            P(None, ("design", "gx"), None, None),
            P(None, ("design", "gx"), None, None),
            P(("design", "gx"), None, None),
            P(None, ("design", "gx"), None, None),
            P(None, None, ("design", "gx"), None),
            P("gx", None),
        ),
        out_specs=(
            P(None, ("design", "gx"), None, None),
            P(None, ("design", "gx"), None, None),
            P(None, ("design", "gx"), None, None),
            P(("design", "gx")),
        ),
        check_vma=False,
    )
```

```python
import functools
import math

import jax
import jax.numpy as jnp
from jax import lax
from jax.experimental import pallas as pl
from jax.experimental.pallas import tpu as pltpu
from jax.sharding import PartitionSpec as P

STEPS = 5
COURANT = 0.5
ANGULAR = 0.3
SENS_SCALE = 0.05
X, Y, Z = 0, 1, 2
VMEM = pl.BlockSpec(memory_space=pltpu.VMEM)
SMEM = pl.BlockSpec(memory_space=pltpu.SMEM)
HBM = pl.BlockSpec(memory_space=pltpu.HBM)


def shifted(field, axis, ahead):
    size = field.shape[axis]
    where = lax.broadcasted_iota(jnp.int32, field.shape, axis)
    if ahead:
        return jnp.where(where == size - 1, 0.0, pltpu.roll(field, size - 1, axis))
    return jnp.where(where == 0, 0.0, pltpu.roll(field, 1, axis))


def magnetic_plane(elec, beyond, mag):
    ex, ey, ez = elec
    curl_x = shifted(ez, 0, True) - ez - (shifted(ey, 1, True) - ey)
    far_y, far_z = beyond if beyond is not None else (0.0, 0.0)
    curl_y = shifted(ex, 1, True) - ex - (far_z - ez)
    curl_z = far_y - ey - (shifted(ex, 0, True) - ex)
    return [
        None if m is None else m - COURANT * c
        for m, c in zip(mag, (curl_x, curl_y, curl_z))
    ]


def electric_plane(mag, before, elec, eps):
    hx, hy, hz = mag
    past_y, past_z = before if before is not None else (0.0, 0.0)
    rot_x = hz - shifted(hz, 0, False) - (hy - shifted(hy, 1, False))
    rot_y = hx - shifted(hx, 1, False) - (hz - past_z)
    rot_z = hy - past_y - (hx - shifted(hx, 0, False))
    half = COURANT * eps
    return [e + half * r for e, r in zip(elec, (rot_x, rot_y, rot_z))]


def planes(ref, p):
    return [ref[c, p] for c in range(3)]


def store(ref, p, values):
    for c, v in enumerate(values):
        ref[c, p] = v


def magnetic_all(elec, mag, count, beyond):
    for p in range(count):
        far = (elec[Y, p + 1], elec[Z, p + 1]) if p + 1 < count else beyond
        store(mag, p, magnetic_plane(planes(elec, p), far, planes(mag, p)))


def electric_all(elec, mag, eps, count, before):
    for p in range(count):
        past = (mag[Y, p - 1], mag[Z, p - 1]) if p else before
        store(elec, p, electric_plane(planes(mag, p), past, planes(elec, p), eps[p]))


def needed(wanted_mag, wanted_elec, count):
    mag, elec = dict(wanted_mag), dict(wanted_elec)
    for step in range(STEPS, 0, -1):
        elec[step] = set(elec.get(step, ()))
        mag[step] = set(mag.get(step, ()))
        mag[step] |= elec[step] | {p - 1 for p in elec[step] if p}
        elec[step - 1] = set(elec.get(step - 1, ())) | elec[step] | mag[step]
        elec[step - 1] |= {p + 1 for p in mag[step] if p + 1 < count}
        mag[step - 1] = set(mag.get(step - 1, ())) | mag[step]
    return mag, elec


def early_kernel(role, own_e, own_m, own_eps, msg, elec, mag):
    count = own_e.shape[1]
    last = count - 1
    even = role[0] == 0

    def run(is_even):
        if is_even:
            want_m, want_e = {}, {1: {0}, 2: {0}}
        else:
            want_m, want_e = {s: {last} for s in range(1, 4)}, {}
        need_m, need_e = needed(want_m, want_e, count)
        for k in range(2):
            msg[6 + k] = own_eps[k if is_even else last - k]
            if is_even:
                msg[k] = own_e[1 + k, 0]
        for step in range(1, 4):
            src_e, src_m = (own_e, own_m) if step == 1 else (elec, mag)
            for p in sorted(need_m[step]):
                far = (src_e[Y, p + 1], src_e[Z, p + 1]) if p < last else None
                new = magnetic_plane(planes(src_e, p), far, planes(src_m, p))
                store(mag, p, new)
                if not is_even and p == last:
                    for k in range(2):
                        msg[2 * step - 2 + k] = new[1 + k]
            for p in sorted(need_e[step]):
                past = (mag[Y, p - 1], mag[Z, p - 1]) if p else None
                new = electric_plane(planes(mag, p), past, planes(src_e, p), own_eps[p])
                store(elec, p, new)
                if is_even and p == 0:
                    for k in range(2):
                        msg[2 * step + k] = new[1 + k]

    pl.when(even)(functools.partial(run, True))
    pl.when(jnp.logical_not(even))(functools.partial(run, False))


def closed_kernel(role, own_e, own_m, own_eps, mate_e, mate_m, mate_eps, msg, nears, elec, mag):
    half = own_e.shape[1]
    count = 2 * half
    even = role[0] == 0

    def send(step, value):
        for k in range(2):
            msg[2 * (step - 4) + k] = value[1 + k]

    def run(is_even):
        steps = range(1, STEPS + 1)
        if is_even:
            want_m, want_e = {}, {s: {0, half} if s > 2 else {half} for s in steps if s < STEPS}
        else:
            want_m, want_e = {s: {half - 1, count - 1} if s > 3 else {half - 1} for s in steps}, {}
        need_m, need_e = needed(want_m, want_e, count)

        def first(own, mate, p):
            ref = own if (p < half) == is_even else mate
            return ref, p % half

        def all_of(step, pair, ref, p):
            if step > 1:
                return planes(ref, p)
            return planes(*first(*pair, p))

        def two_of(step, pair, ref, p):
            return tuple(all_of(step, pair, ref, p)[1:])

        pair_e, pair_m = (own_e, mate_e), (own_m, mate_m)
        if is_even:
            for k in range(2):
                nears[k] = mate_e[1 + k, 0]
        for step in steps:
            for p in sorted(need_m[step]):
                far = two_of(step, pair_e, elec, p + 1) if p + 1 < count else None
                here = all_of(step, pair_e, elec, p)
                new = magnetic_plane(here, far, all_of(step, pair_m, mag, p))
                store(mag, p, new)
                if not is_even and p == count - 1 and step > 3:
                    send(step, new)
                if not is_even and p == half - 1:
                    nears[2 * (step - 1)] = new[Y] - COURANT * far[1]
                    nears[2 * (step - 1) + 1] = new[Z] + COURANT * far[0]
            for p in sorted(need_e[step]):
                past = (mag[Y, p - 1], mag[Z, p - 1]) if p else None
                ref, at = first(own_eps, mate_eps, p)
                new = electric_plane(planes(mag, p), past, all_of(step, pair_e, elec, p), ref[at])
                store(elec, p, new)
                if is_even and p == 0 and step > 2:
                    send(step + 1, new)
                if is_even and p == half:
                    for k in range(2):
                        nears[2 * step + k] = new[1 + k]

    pl.when(even)(functools.partial(run, True))
    pl.when(jnp.logical_not(even))(functools.partial(run, False))


def past_near(near, elec):
    return (near[0] + COURANT * elec[Z, 0], near[1] - COURANT * elec[Y, 0])


def weights_kernel(forward, weights):
    depth, count, ny = forward.shape[1:]
    nz = weights.shape[3]
    blank = jnp.zeros(((nz - depth) // 2, ny), jnp.float32)
    for p in range(count):
        for c in range(6):
            slab = forward[c, :, p, :] * (SENS_SCALE if c < 3 else -SENS_SCALE)
            weights[c, p] = jnp.transpose(jnp.concatenate([blank, slab, blank], 0))


LEFT_MAG = {1: 1, 2: 2, 3: 3, 4: 2, 5: 1}
LEFT_ELEC = {1: 1, 2: 2, 3: 2, 4: 1, 5: 0}
RIGHT_MAG = {1: 0, 2: 1, 3: 2, 4: 1, 5: 0}
RIGHT_ELEC = {1: 1, 2: 2, 3: 2, 4: 1, 5: 0}


def beyond_left(step, elec, side_e, side_m):
    for j in range(LEFT_MAG[step]):
        if j == 0:
            far = (elec[Y, 0], elec[Z, 0])
        else:
            far = (side_e[Y, j - 1], side_e[Z, j - 1])
        store(side_m, j, magnetic_plane(planes(side_e, j), far, planes(side_m, j)))


def beyond_left_electric(step, side_e, side_m, side_eps):
    for j in range(LEFT_ELEC[step]):
        past = (side_m[Y, j + 1], side_m[Z, j + 1])
        store(side_e, j, electric_plane(planes(side_m, j), past, planes(side_e, j), side_eps[j]))


def beyond_right(step, mag, side_e, side_m, side_eps, last):
    for j in range(RIGHT_MAG[step]):
        far = (side_e[Y, j + 1], side_e[Z, j + 1])
        store(side_m, j, magnetic_plane(planes(side_e, j), far, planes(side_m, j)))
    for j in range(RIGHT_ELEC[step]):
        if j == 0:
            past = (mag[Y, last], mag[Z, last])
        else:
            past = (side_m[Y, j - 1], side_m[Z, j - 1])
        store(side_e, j, electric_plane(planes(side_m, j), past, planes(side_e, j), side_eps[j]))


def open_kernel(steps, role, elec_in, mag_in, eps, nears, opening, *refs):
    ending = steps[-1] == STEPS
    if ending:
        msgs, accum_in, late_in, side_e_in, side_m_in, weights, high, low = refs[:8]
        elec_out, mag_out, accum_out, pillars, elec, mag, accum, side_e, side_m, sems = refs[8:]
    else:
        accum_in, elec, mag, accum, side_e, side_m, late = refs
    count = eps.shape[0]
    last = count - 1
    even = role[0] == 0
    side_eps = opening.at[6:8]
    for ref, from_ref in zip((side_e, side_m), (side_e_in, side_m_in) if ending else (None, None)):
        for j in range(2):
            for c in range(3):
                ref[c, j] = jnp.zeros(eps.shape[1:], jnp.float32) if from_ref is None else from_ref[c, j]
    if not ending:
        for c in range(3):
            side_e[c, 2] = jnp.zeros(eps.shape[1:], jnp.float32)
            side_m[c, 2] = jnp.zeros(eps.shape[1:], jnp.float32)

    pending = []

    def put(src, dst):
        copy = pltpu.make_async_copy(src, dst, sems.at[len(pending)])
        copy.start()
        pending.append(copy)

    def run(is_even):
        pending.clear()
        sums = None
        scale = role[1 if is_even else 2].astype(jnp.float32)
        if not ending:
            far = (opening[0], opening[1])
            if is_even:
                far = past_near(far, elec_in)
            factor = scale
            for p in range(count):
                factor = factor * (COURANT * COURANT * eps[p])
            for k in range(2):
                late[k] = factor * far[k]
        for step in steps:
            src_e, src_m = (elec_in, mag_in) if step == steps[0] else (elec, mag)
            near = (nears[2 * step - 2], nears[2 * step - 1])
            if step == STEPS:
                near = (near[0] + late_in[0], near[1] + late_in[1])
            ref, at = (opening, 2 * step - 2) if step < 4 else (msgs, 2 * step - 8)
            far = (ref[at], ref[at + 1])
            if is_even:
                beyond = near
                beyond_left(step, src_e, side_e, side_m)
                past0 = ((far[0] + side_m[Y, 0]) * scale, (far[1] + side_m[Z, 0]) * scale)
            else:
                beyond = ((far[0] + side_e[Y, 0]) * scale, (far[1] + side_e[Z, 0]) * scale)
                past0 = past_near(near, src_e)
            for p in range(count):
                nxt = (src_e[Y, p + 1], src_e[Z, p + 1]) if p < last else beyond
                store(mag, p, magnetic_plane(planes(src_e, p), nxt, planes(src_m, p)))
            if step == STEPS:
                put(mag, mag_out)
            if is_even:
                beyond_left_electric(step, side_e, side_m, side_eps)
            else:
                beyond_right(step, mag, side_e, side_m, side_eps, last)
            waves = (math.cos(ANGULAR * step), math.sin(ANGULAR * step))
            src_a = accum_in if step == steps[0] else accum
            for p in range(count):
                past = (mag[Y, p - 1], mag[Z, p - 1]) if p else past0
                new = electric_plane(planes(mag, p), past, planes(src_e, p), eps[p])
                store(elec, p, new)
                total = None
                for c in range(6):
                    value = src_a[c, p] + waves[c // 3] * new[c % 3]
                    accum[c, p] = value
                    if step == STEPS:
                        term = value * weights[c, p]
                        total = term if total is None else total + term
                if step == STEPS:
                    put(elec.at[:, p], elec_out.at[:, p])
                    put(accum.at[:, p], accum_out.at[:, p])
                    term = pillar_terms(total, high[p : p + 1], low[p], pillars.shape[0])
                    sums = term if sums is None else sums + term
        if ending:
            pillars[...] = sums
        for copy in pending:
            copy.wait()

    pl.when(even)(functools.partial(run, True))
    pl.when(jnp.logical_not(even))(functools.partial(run, False))


def pillar_terms(total, high, low, owners):
    row = lax.dot_general(
        jnp.ones((8, total.shape[1]), jnp.float32), total, (((1,), (1,)), ((), ())),
        precision=lax.Precision.HIGHEST, preferred_element_type=jnp.float32,
    )[0:1]
    label = lax.broadcasted_iota(jnp.int32, (owners, total.shape[0]), 0)
    return lax.dot_general(
        jnp.where(label == high, row, 0.0), low, (((1,), (0,)), ((), ())),
        precision=lax.Precision.HIGHEST, preferred_element_type=jnp.float32,
    )


def call(kernel, args, outs, scratch=(), smem=1, fast=(), slow_outs=0, copies=0):
    args = [
        pltpu.with_memory_space_constraint(a, pltpu.VMEM if i in fast else pltpu.HBM) if i >= smem else a
        for i, a in enumerate(args)
    ]
    return pl.pallas_call(
        kernel,
        out_shape=[
            shape_of(*o) if i < slow_outs else pltpu.VMEM(o, jnp.float32) for i, o in enumerate(outs)
        ],
        in_specs=[SMEM] * smem + [VMEM] * (len(args) - smem),
        out_specs=[HBM] * slow_outs + [VMEM] * (len(outs) - slow_outs),
        scratch_shapes=[pltpu.VMEM(d, jnp.float32) for d in scratch]
        + [pltpu.SemaphoreType.DMA((copies,))] * (copies > 0),
        compiler_params=pltpu.CompilerParams(vmem_limit_bytes=12 * 2**20),
        cost_estimate=pl.CostEstimate(flops=1, bytes_accessed=1, transcendentals=0),
    )(*args)


def shape_of(*dims):
    return jax.ShapeDtypeStruct(dims, jnp.float32)


def halved(sums, axis):
    size = lax.axis_size(axis)
    me = lax.axis_index(axis)
    bits = size.bit_length() - 1
    block = sums
    for bit in range(bits):
        pair = block.reshape(-1, 2, block.shape[-1])
        mine = (me >> bit) & 1
        keep = jnp.where(mine == 0, pair[:, 0], pair[:, 1])
        give = jnp.where(mine == 0, pair[:, 1], pair[:, 0])
        block = keep + lax.ppermute(give, axis, [(i, i ^ (1 << bit)) for i in range(size)])
    return block.reshape(-1)


def per_device(electric, magnetic, inv_eps, accum, forward, pillar_ids):
    size = lax.axis_size("gx")
    me = lax.axis_index("gx")
    role = jnp.stack([me % 2, jnp.where(me == 0, 0, 1), jnp.where(me == size - 1, 0, 1)]).astype(jnp.int32)
    count, ny, nz = inv_eps.shape
    same_chip = [(i, i ^ 1) for i in range(size)]
    inner = range(1, size - 1, 2)
    next_chip = [(i, i + 1) for i in inner] + [(i + 1, i) for i in inner]

    per_owner = ny
    high = pillar_ids // per_owner
    low = (pillar_ids % per_owner)[:, :, None] == jnp.arange(per_owner, dtype=jnp.int32)
    low = low.astype(jnp.float32)
    field, side = electric.shape, (3, 3, ny, nz)

    def to_mate(block):
        return lax.ppermute(block, "gx", same_chip)

    def to_chip(block):
        return lax.ppermute(block, "gx", next_chip)

    own = [role, electric, magnetic, inv_eps]
    (opening,) = call(early_kernel, own, [(8, ny, nz)], scratch=[field, field])
    opening = to_chip(opening)
    mate = [to_mate(electric), to_mate(magnetic), to_mate(inv_eps)]
    later, nears = call(
        closed_kernel,
        own + mate,
        [(4, ny, nz), (2 * STEPS, ny, nz)],
        scratch=[(3, 2 * count, ny, nz)] * 2,
        fast=(4, 5, 6),
    )
    later = to_chip(later)
    (weights,) = call(weights_kernel, [forward], [accum.shape], smem=0)
    elec, mag, total, side_e, side_m, late = call(
        functools.partial(open_kernel, (1, 2, 3)),
        own + [nears, opening, accum],
        [field, field, accum.shape, side, side, (2, ny, nz)],
        fast=(4, 5),
    )
    late = to_mate(late)
    electric, magnetic, accum, sums = call(
        functools.partial(open_kernel, (4, 5)),
        [role, elec, mag, inv_eps, nears, opening, later, total, late, side_e, side_m, weights, high, low],
        [field, field, accum.shape, (size, per_owner)],
        scratch=[field, field, accum.shape, side, side],
        fast=(1, 2, *range(4, 12)),
        slow_outs=3,
        copies=1 + 2 * count,
    )
    return electric, magnetic, accum, halved(sums, "gx")


def solution(mesh):
    return jax.shard_map(
        per_device,
        mesh=mesh,
        in_specs=(
            P(None, ("design", "gx"), None, None),
            P(None, ("design", "gx"), None, None),
            P(("design", "gx"), None, None),
            P(None, ("design", "gx"), None, None),
            P(None, None, ("design", "gx"), None),
            P("gx", None),
        ),
        out_specs=(
            P(None, ("design", "gx"), None, None),
            P(None, ("design", "gx"), None, None),
            P(None, ("design", "gx"), None, None),
            P(("design", "gx")),
        ),
        check_vma=False,
    )
```

```python
import functools
import math

import jax
import jax.numpy as jnp
from jax import lax
from jax.experimental import pallas as pl
from jax.experimental.pallas import tpu as pltpu
from jax.sharding import PartitionSpec as P

STEPS = 5
COURANT = 0.5
ANGULAR = 0.3
SENS_SCALE = 0.05
X, Y, Z = 0, 1, 2
VMEM = pl.BlockSpec(memory_space=pltpu.VMEM)
SMEM = pl.BlockSpec(memory_space=pltpu.SMEM)
HBM = pl.BlockSpec(memory_space=pltpu.HBM)


def shifted(field, axis, ahead):
    size = field.shape[axis]
    where = lax.broadcasted_iota(jnp.int32, field.shape, axis)
    if ahead:
        return jnp.where(where == size - 1, 0.0, pltpu.roll(field, size - 1, axis))
    return jnp.where(where == 0, 0.0, pltpu.roll(field, 1, axis))


def magnetic_plane(elec, beyond, mag):
    ex, ey, ez = elec
    curl_x = shifted(ez, 0, True) - ez - (shifted(ey, 1, True) - ey)
    far_y, far_z = beyond if beyond is not None else (0.0, 0.0)
    curl_y = shifted(ex, 1, True) - ex - (far_z - ez)
    curl_z = far_y - ey - (shifted(ex, 0, True) - ex)
    return [
        None if m is None else m - COURANT * c
        for m, c in zip(mag, (curl_x, curl_y, curl_z))
    ]


def electric_plane(mag, before, elec, eps):
    hx, hy, hz = mag
    past_y, past_z = before if before is not None else (0.0, 0.0)
    rot_x = hz - shifted(hz, 0, False) - (hy - shifted(hy, 1, False))
    rot_y = hx - shifted(hx, 1, False) - (hz - past_z)
    rot_z = hy - past_y - (hx - shifted(hx, 0, False))
    half = COURANT * eps
    return [e + half * r for e, r in zip(elec, (rot_x, rot_y, rot_z))]


def planes(ref, p):
    return [ref[c, p] for c in range(3)]


def store(ref, p, values):
    for c, v in enumerate(values):
        ref[c, p] = v


def magnetic_all(elec, mag, count, beyond):
    for p in range(count):
        far = (elec[Y, p + 1], elec[Z, p + 1]) if p + 1 < count else beyond
        store(mag, p, magnetic_plane(planes(elec, p), far, planes(mag, p)))


def electric_all(elec, mag, eps, count, before):
    for p in range(count):
        past = (mag[Y, p - 1], mag[Z, p - 1]) if p else before
        store(elec, p, electric_plane(planes(mag, p), past, planes(elec, p), eps[p]))


def needed(wanted_mag, wanted_elec, count):
    mag, elec = dict(wanted_mag), dict(wanted_elec)
    for step in range(STEPS, 0, -1):
        elec[step] = set(elec.get(step, ()))
        mag[step] = set(mag.get(step, ()))
        mag[step] |= elec[step] | {p - 1 for p in elec[step] if p}
        elec[step - 1] = set(elec.get(step - 1, ())) | elec[step] | mag[step]
        elec[step - 1] |= {p + 1 for p in mag[step] if p + 1 < count}
        mag[step - 1] = set(mag.get(step - 1, ())) | mag[step]
    return mag, elec


def early_kernel(role, own_e, own_m, own_eps, msg_a, msg_b, elec, mag):
    count = own_e.shape[1]
    last = count - 1
    even = role[0] == 0

    def send(step, value):
        ref = msg_a if step < 3 else msg_b
        for k in range(2):
            ref[2 * ((step - 1) % 2) + k] = value[1 + k]

    def run(is_even):
        if is_even:
            want_m, want_e = {}, {s: {0} for s in range(1, 4)}
        else:
            want_m, want_e = {s: {last} for s in range(1, 5)}, {}
        need_m, need_e = needed(want_m, want_e, count)
        for k in range(2):
            msg_a[4 + k] = own_eps[k if is_even else last - k]
        if is_even:
            send(1, planes(own_e, 0))
        for step in range(1, 5):
            src_e, src_m = (own_e, own_m) if step == 1 else (elec, mag)
            for p in sorted(need_m[step]):
                far = (src_e[Y, p + 1], src_e[Z, p + 1]) if p < last else None
                new = magnetic_plane(planes(src_e, p), far, planes(src_m, p))
                store(mag, p, new)
                if not is_even and p == last:
                    send(step, new)
            for p in sorted(need_e[step]):
                past = (mag[Y, p - 1], mag[Z, p - 1]) if p else None
                new = electric_plane(planes(mag, p), past, planes(src_e, p), own_eps[p])
                store(elec, p, new)
                if is_even and p == 0:
                    send(step + 1, new)

    pl.when(even)(functools.partial(run, True))
    pl.when(jnp.logical_not(even))(functools.partial(run, False))


def closed_kernel(role, own_e, own_m, own_eps, mate_e, mate_m, mate_eps, msg, nears, elec, mag):
    half = own_e.shape[1]
    count = 2 * half
    even = role[0] == 0

    def send(value):
        for k in range(2):
            msg[k] = value[1 + k]

    def run(is_even):
        steps = range(1, STEPS + 1)
        if is_even:
            want_m, want_e = {}, {s: {0, half} if s > 3 else {half} for s in steps if s < STEPS}
        else:
            want_m, want_e = {s: {half - 1, count - 1} if s > 4 else {half - 1} for s in steps}, {}
        need_m, need_e = needed(want_m, want_e, count)

        def first(own, mate, p):
            ref = own if (p < half) == is_even else mate
            return ref, p % half

        def all_of(step, pair, ref, p):
            if step > 1:
                return planes(ref, p)
            return planes(*first(*pair, p))

        def two_of(step, pair, ref, p):
            return tuple(all_of(step, pair, ref, p)[1:])

        pair_e, pair_m = (own_e, mate_e), (own_m, mate_m)
        if is_even:
            for k in range(2):
                nears[k] = mate_e[1 + k, 0]
        for step in steps:
            for p in sorted(need_m[step]):
                far = two_of(step, pair_e, elec, p + 1) if p + 1 < count else None
                here = all_of(step, pair_e, elec, p)
                new = magnetic_plane(here, far, all_of(step, pair_m, mag, p))
                store(mag, p, new)
                if not is_even and p == count - 1 and step == STEPS:
                    send(new)
                if not is_even and p == half - 1:
                    nears[2 * (step - 1)] = new[Y] - COURANT * far[1]
                    nears[2 * (step - 1) + 1] = new[Z] + COURANT * far[0]
            for p in sorted(need_e[step]):
                past = (mag[Y, p - 1], mag[Z, p - 1]) if p else None
                ref, at = first(own_eps, mate_eps, p)
                new = electric_plane(planes(mag, p), past, all_of(step, pair_e, elec, p), ref[at])
                store(elec, p, new)
                if is_even and p == 0 and step == STEPS - 1:
                    send(new)
                if is_even and p == half:
                    for k in range(2):
                        nears[2 * step + k] = new[1 + k]

    pl.when(even)(functools.partial(run, True))
    pl.when(jnp.logical_not(even))(functools.partial(run, False))


def past_near(near, elec):
    return (near[0] + COURANT * elec[Z, 0], near[1] - COURANT * elec[Y, 0])


def staging_kernel(forward, *refs):
    half = (len(refs) - 2) // 2
    sems, weights = refs[-1], refs[half]
    copies = [
        pltpu.make_async_copy(refs[i], refs[half + 1 + i], sems.at[i]) for i in range(half)
    ]
    for copy in copies:
        copy.start()
    depth, count, ny = forward.shape[1:]
    nz = weights.shape[3]
    blank = jnp.zeros(((nz - depth) // 2, ny), jnp.float32)
    for p in range(count):
        for c in range(6):
            slab = forward[c, :, p, :] * (SENS_SCALE if c < 3 else -SENS_SCALE)
            weights[c, p] = jnp.transpose(jnp.concatenate([blank, slab, blank], 0))
    for copy in copies:
        copy.wait()


LEFT_MAG = {1: 1, 2: 2, 3: 3, 4: 2, 5: 1}
LEFT_ELEC = {1: 1, 2: 2, 3: 2, 4: 1, 5: 0}
RIGHT_MAG = {1: 0, 2: 1, 3: 2, 4: 1, 5: 0}
RIGHT_ELEC = {1: 1, 2: 2, 3: 2, 4: 1, 5: 0}


def beyond_left(step, elec, side_e, side_m):
    for j in range(LEFT_MAG[step]):
        if j == 0:
            far = (elec[Y, 0], elec[Z, 0])
        else:
            far = (side_e[Y, j - 1], side_e[Z, j - 1])
        store(side_m, j, magnetic_plane(planes(side_e, j), far, planes(side_m, j)))


def beyond_left_electric(step, side_e, side_m, side_eps):
    for j in range(LEFT_ELEC[step]):
        past = (side_m[Y, j + 1], side_m[Z, j + 1])
        store(side_e, j, electric_plane(planes(side_m, j), past, planes(side_e, j), side_eps[j]))


def beyond_right(step, mag, side_e, side_m, side_eps, last):
    for j in range(RIGHT_MAG[step]):
        far = (side_e[Y, j + 1], side_e[Z, j + 1])
        store(side_m, j, magnetic_plane(planes(side_e, j), far, planes(side_m, j)))
    for j in range(RIGHT_ELEC[step]):
        if j == 0:
            past = (mag[Y, last], mag[Z, last])
        else:
            past = (side_m[Y, j - 1], side_m[Z, j - 1])
        store(side_e, j, electric_plane(planes(side_m, j), past, planes(side_e, j), side_eps[j]))


def open_kernel(steps, *refs):
    first, ending = steps[0], steps[-1] == STEPS
    names = ["role", "elec_in", "mag_in", "eps", "nears", "opening", "accum_in"]
    names += ["msgs", "side_e_in", "side_m_in"] * (first > 1)
    names += ["late_in", "weights", "ids"] * ending
    names += ["elec_out", "mag_out", "accum_out", "pillars"] * ending
    names += ["elec", "mag", "accum", "side_e", "side_m"]
    names += ["late"] * (first == 1) + ["sems"] * ending
    r = dict(zip(names, refs, strict=True))
    role, elec_in, mag_in, eps, nears, opening, accum_in = refs[:7]
    elec, mag, accum, side_e, side_m = (r[n] for n in ("elec", "mag", "accum", "side_e", "side_m"))
    count = eps.shape[0]
    last = count - 1
    even = role[0] == 0
    side_eps = opening.at[4:6]
    reached = min(first - 1, STEPS + 1 - first)
    for j in range(3):
        for c in range(3):
            if j < reached:
                side_e[c, j] = r["side_e_in"][c, j]
                side_m[c, j] = r["side_m_in"][c, j]
            elif first < STEPS:
                side_e[c, j] = jnp.zeros(eps.shape[1:], jnp.float32)
                side_m[c, j] = jnp.zeros(eps.shape[1:], jnp.float32)

    pending = []

    def put(src, dst):
        copy = pltpu.make_async_copy(src, dst, r["sems"].at[len(pending)])
        copy.start()
        pending.append(copy)

    def run(is_even):
        pending.clear()
        sums = None
        scale = role[1 if is_even else 2].astype(jnp.float32)
        if first == 1:
            far = (opening[0], opening[1])
            if is_even:
                far = past_near(far, elec_in)
            factor = scale
            for p in range(count):
                factor = factor * (COURANT * COURANT * eps[p])
            for k in range(2):
                r["late"][k] = factor * far[k]
        for step in steps:
            src_e, src_m = (elec_in, mag_in) if step == steps[0] else (elec, mag)
            near = (nears[2 * step - 2], nears[2 * step - 1])
            if step == STEPS:
                near = (near[0] + r["late_in"][0], near[1] + r["late_in"][1])
            ref, at = (opening if step < 3 else r["msgs"]), 2 * ((step - 1) % 2)
            far = (ref[at], ref[at + 1])
            if is_even:
                beyond = near
                beyond_left(step, src_e, side_e, side_m)
                past0 = ((far[0] + side_m[Y, 0]) * scale, (far[1] + side_m[Z, 0]) * scale)
            else:
                beyond = ((far[0] + side_e[Y, 0]) * scale, (far[1] + side_e[Z, 0]) * scale)
                past0 = past_near(near, src_e)
            for p in range(count):
                nxt = (src_e[Y, p + 1], src_e[Z, p + 1]) if p < last else beyond
                store(mag, p, magnetic_plane(planes(src_e, p), nxt, planes(src_m, p)))
            if step == STEPS:
                put(mag, r["mag_out"])
            if is_even:
                beyond_left_electric(step, side_e, side_m, side_eps)
            else:
                beyond_right(step, mag, side_e, side_m, side_eps, last)
            waves = (math.cos(ANGULAR * step), math.sin(ANGULAR * step))
            src_a = accum_in if step == steps[0] else accum
            for p in range(count):
                past = (mag[Y, p - 1], mag[Z, p - 1]) if p else past0
                new = electric_plane(planes(mag, p), past, planes(src_e, p), eps[p])
                store(elec, p, new)
                total = None
                for c in range(6):
                    value = src_a[c, p] + waves[c // 3] * new[c % 3]
                    accum[c, p] = value
                    if step == STEPS:
                        term = value * r["weights"][c, p]
                        total = term if total is None else total + term
                if step == STEPS:
                    put(elec.at[:, p], r["elec_out"].at[:, p])
                    put(accum.at[:, p], r["accum_out"].at[:, p])
                    term = pillar_terms(total, r["ids"][p : p + 1], r["pillars"].shape[0])
                    sums = term if sums is None else sums + term
        if ending:
            r["pillars"][...] = sums
        for copy in pending:
            copy.wait()

    pl.when(even)(functools.partial(run, True))
    pl.when(jnp.logical_not(even))(functools.partial(run, False))


def pillar_terms(total, ids, owners):
    row = lax.dot_general(
        jnp.ones((8, total.shape[1]), jnp.float32), total, (((1,), (1,)), ((), ())),
        precision=lax.Precision.HIGHEST, preferred_element_type=jnp.float32,
    )[0:1]
    each = total.shape[0]
    owner = lax.broadcasted_iota(jnp.int32, (owners, each), 0)
    label = lax.broadcasted_iota(jnp.int32, (each, each), 0)
    high = lax.div(ids, jnp.int32(each))
    return lax.dot_general(
        jnp.where(owner == high, row, 0.0),
        jnp.where(label == ids - each * high, 1.0, 0.0),
        (((1,), (1,)), ((), ())),
        precision=lax.Precision.HIGHEST, preferred_element_type=jnp.float32,
    )


def call(kernel, args, outs, scratch=(), smem=1, fast=(), slow_outs=0, copies=0, slow=()):
    args = [
        pltpu.with_memory_space_constraint(a, pltpu.VMEM if i in fast else pltpu.HBM) if i >= smem else a
        for i, a in enumerate(args)
    ]
    return pl.pallas_call(
        kernel,
        out_shape=[
            shape_of(*o) if i < slow_outs else pltpu.VMEM(o, jnp.float32) for i, o in enumerate(outs)
        ],
        in_specs=[SMEM if i < smem else HBM if i in slow else VMEM for i in range(len(args))],
        out_specs=[HBM] * slow_outs + [VMEM] * (len(outs) - slow_outs),
        scratch_shapes=[pltpu.VMEM(d, jnp.float32) for d in scratch]
        + [pltpu.SemaphoreType.DMA((copies,))] * (copies > 0),
        compiler_params=pltpu.CompilerParams(vmem_limit_bytes=12 * 2**20),
        cost_estimate=pl.CostEstimate(flops=1, bytes_accessed=1, transcendentals=0),
    )(*args)


def shape_of(*dims):
    return jax.ShapeDtypeStruct(dims, jnp.float32)


def summed(sums):
    return jnp.sum(lax.all_to_all(sums, "gx", 0, 0, tiled=True), 0)


def per_device(electric, magnetic, inv_eps, accum, forward, pillar_ids):
    size = lax.axis_size("gx")
    me = lax.axis_index("gx")
    role = jnp.stack([me % 2, jnp.where(me == 0, 0, 1), jnp.where(me == size - 1, 0, 1)]).astype(jnp.int32)
    count, ny, nz = inv_eps.shape
    same_chip = [(i, i ^ 1) for i in range(size)]
    inner = range(1, size - 1, 2)
    next_chip = [(i, i + 1) for i in inner] + [(i + 1, i) for i in inner]

    field, side = electric.shape, (3, 3, ny, nz)

    def to_mate(block):
        return lax.ppermute(block, "gx", same_chip)

    def to_chip(block):
        return lax.ppermute(block, "gx", next_chip)

    own = [role, electric, magnetic, inv_eps]
    opening, middle = call(
        early_kernel, own, [(6, ny, nz), (4, ny, nz)], scratch=[field, field]
    )
    opening = to_chip(opening)
    middle = to_chip(middle)
    mate = [to_mate(electric), to_mate(magnetic), to_mate(inv_eps)]
    ending, nears = call(
        closed_kernel,
        own + mate,
        [(2, ny, nz), (2 * STEPS, ny, nz)],
        scratch=[(3, 2 * count, ny, nz)] * 2,
        fast=(4, 5, 6),
    )
    ending = to_chip(ending)
    weights, elec, mag, eps, total = call(
        staging_kernel,
        [forward, electric, magnetic, inv_eps, accum],
        [accum.shape, field, field, inv_eps.shape, accum.shape],
        smem=0,
        slow=(1, 2, 3, 4),
        copies=4,
    )
    kept = [field, field, accum.shape, side, side]
    elec, mag, total, *sides, late = call(
        functools.partial(open_kernel, (1, 2)),
        [role, elec, mag, eps, nears, opening, total],
        kept + [(2, ny, nz)],
        fast=range(1, 7),
    )
    late = to_mate(late)
    elec, mag, total, *sides = call(
        functools.partial(open_kernel, (3, 4)),
        [role, elec, mag, eps, nears, opening, total, middle, *sides],
        kept,
        fast=range(1, 10),
    )
    electric, magnetic, accum, sums = call(
        functools.partial(open_kernel, (5,)),
        [role, elec, mag, eps, nears, opening, total, ending, *sides, late, weights, pillar_ids],
        [field, field, accum.shape, (size, ny)],
        scratch=kept,
        fast=range(1, 12),
        slow_outs=3,
        copies=1 + 2 * count,
    )
    return electric, magnetic, accum, summed(sums)


def solution(mesh):
    return jax.shard_map(
        per_device,
        mesh=mesh,
        in_specs=(
            P(None, ("design", "gx"), None, None),
            P(None, ("design", "gx"), None, None),
            P(("design", "gx"), None, None),
            P(None, ("design", "gx"), None, None),
            P(None, None, ("design", "gx"), None),
            P("gx", None),
        ),
        out_specs=(
            P(None, ("design", "gx"), None, None),
            P(None, ("design", "gx"), None, None),
            P(None, ("design", "gx"), None, None),
            P(("design", "gx")),
        ),
        check_vma=False,
    )
```

```python
import functools
import math

import jax
import jax.numpy as jnp
from jax import lax
from jax.experimental import pallas as pl
from jax.experimental.pallas import tpu as pltpu
from jax.sharding import PartitionSpec as P

STEPS = 5
COURANT = 0.5
ANGULAR = 0.3
SENS_SCALE = 0.05
X, Y, Z = 0, 1, 2
VMEM = pl.BlockSpec(memory_space=pltpu.VMEM)
SMEM = pl.BlockSpec(memory_space=pltpu.SMEM)
HBM = pl.BlockSpec(memory_space=pltpu.HBM)


def shifted(field, axis, ahead):
    size = field.shape[axis]
    where = lax.broadcasted_iota(jnp.int32, field.shape, axis)
    if ahead:
        return jnp.where(where == size - 1, 0.0, pltpu.roll(field, size - 1, axis))
    return jnp.where(where == 0, 0.0, pltpu.roll(field, 1, axis))


def magnetic_plane(elec, beyond, mag):
    ex, ey, ez = elec
    curl_x = shifted(ez, 0, True) - ez - (shifted(ey, 1, True) - ey)
    far_y, far_z = beyond if beyond is not None else (0.0, 0.0)
    curl_y = shifted(ex, 1, True) - ex - (far_z - ez)
    curl_z = far_y - ey - (shifted(ex, 0, True) - ex)
    return [
        None if m is None else m - COURANT * c
        for m, c in zip(mag, (curl_x, curl_y, curl_z))
    ]


def electric_plane(mag, before, elec, eps):
    hx, hy, hz = mag
    past_y, past_z = before if before is not None else (0.0, 0.0)
    rot_x = hz - shifted(hz, 0, False) - (hy - shifted(hy, 1, False))
    rot_y = hx - shifted(hx, 1, False) - (hz - past_z)
    rot_z = hy - past_y - (hx - shifted(hx, 0, False))
    half = COURANT * eps
    return [e + half * r for e, r in zip(elec, (rot_x, rot_y, rot_z))]


def planes(ref, p):
    return [ref[c, p] for c in range(3)]


def store(ref, p, values):
    for c, v in enumerate(values):
        ref[c, p] = v


def magnetic_all(elec, mag, count, beyond):
    for p in range(count):
        far = (elec[Y, p + 1], elec[Z, p + 1]) if p + 1 < count else beyond
        store(mag, p, magnetic_plane(planes(elec, p), far, planes(mag, p)))


def electric_all(elec, mag, eps, count, before):
    for p in range(count):
        past = (mag[Y, p - 1], mag[Z, p - 1]) if p else before
        store(elec, p, electric_plane(planes(mag, p), past, planes(elec, p), eps[p]))


def needed(wanted_mag, wanted_elec, count):
    mag, elec = dict(wanted_mag), dict(wanted_elec)
    for step in range(STEPS, 0, -1):
        elec[step] = set(elec.get(step, ()))
        mag[step] = set(mag.get(step, ()))
        mag[step] |= elec[step] | {p - 1 for p in elec[step] if p}
        elec[step - 1] = set(elec.get(step - 1, ())) | elec[step] | mag[step]
        elec[step - 1] |= {p + 1 for p in mag[step] if p + 1 < count}
        mag[step - 1] = set(mag.get(step - 1, ())) | mag[step]
    return mag, elec


def parts(block):
    return block.at[0:3], block.at[3:6], block.at[6]


def early_kernel(role, own_e, own_m, own_eps, msg_a, msg_b, elec, mag):
    count = own_e.shape[1]
    last = count - 1
    even = role[0] == 0

    def send(step, value):
        ref = msg_a if step < 3 else msg_b
        for k in range(2):
            ref[2 * ((step - 1) % 2) + k] = value[1 + k]

    def run(is_even):
        if is_even:
            want_m, want_e = {}, {s: {0} for s in range(1, 4)}
        else:
            want_m, want_e = {s: {last} for s in range(1, 5)}, {}
        need_m, need_e = needed(want_m, want_e, count)
        for k in range(2):
            msg_a[4 + k] = own_eps[k if is_even else last - k]
        if is_even:
            send(1, planes(own_e, 0))
        for step in range(1, 5):
            src_e, src_m = (own_e, own_m) if step == 1 else (elec, mag)
            for p in sorted(need_m[step]):
                far = (src_e[Y, p + 1], src_e[Z, p + 1]) if p < last else None
                new = magnetic_plane(planes(src_e, p), far, planes(src_m, p))
                store(mag, p, new)
                if not is_even and p == last:
                    send(step, new)
            for p in sorted(need_e[step]):
                past = (mag[Y, p - 1], mag[Z, p - 1]) if p else None
                new = electric_plane(planes(mag, p), past, planes(src_e, p), own_eps[p])
                store(elec, p, new)
                if is_even and p == 0:
                    send(step + 1, new)

    pl.when(even)(functools.partial(run, True))
    pl.when(jnp.logical_not(even))(functools.partial(run, False))


def closed_kernel(role, mate_e, mate_m, mate_eps, *refs):
    sources, (block, msg, nears, weights, total, elec, mag, forward, sems) = refs[:5], refs[5:]
    own_e, own_m, own_eps = parts(block)
    copies = [
        pltpu.make_async_copy(src, dst, sems.at[i])
        for i, (src, dst) in enumerate(zip(sources, (own_e, own_m, own_eps, forward, total)))
    ]
    for copy in copies:
        copy.start()
    for copy in copies[:3]:
        copy.wait()
    half = own_e.shape[1]
    count = 2 * half
    even = role[0] == 0

    def send(value):
        for k in range(2):
            msg[k] = value[1 + k]

    def run(is_even):
        steps = range(1, STEPS + 1)
        if is_even:
            want_m, want_e = {}, {s: {0, half} if s > 3 else {half} for s in steps if s < STEPS}
        else:
            want_m, want_e = {s: {half - 1, count - 1} if s > 4 else {half - 1} for s in steps}, {}
        need_m, need_e = needed(want_m, want_e, count)

        def first(own, mate, p):
            ref = own if (p < half) == is_even else mate
            return ref, p % half

        def all_of(step, pair, ref, p):
            if step > 1:
                return planes(ref, p)
            return planes(*first(*pair, p))

        def two_of(step, pair, ref, p):
            return tuple(all_of(step, pair, ref, p)[1:])

        pair_e, pair_m = (own_e, mate_e), (own_m, mate_m)
        if is_even:
            for k in range(2):
                nears[k] = mate_e[1 + k, 0]
        for step in steps:
            for p in sorted(need_m[step]):
                far = two_of(step, pair_e, elec, p + 1) if p + 1 < count else None
                here = all_of(step, pair_e, elec, p)
                new = magnetic_plane(here, far, all_of(step, pair_m, mag, p))
                store(mag, p, new)
                if not is_even and p == count - 1 and step == STEPS:
                    send(new)
                if not is_even and p == half - 1:
                    nears[2 * (step - 1)] = new[Y] - COURANT * far[1]
                    nears[2 * (step - 1) + 1] = new[Z] + COURANT * far[0]
            for p in sorted(need_e[step]):
                past = (mag[Y, p - 1], mag[Z, p - 1]) if p else None
                ref, at = first(own_eps, mate_eps, p)
                new = electric_plane(planes(mag, p), past, all_of(step, pair_e, elec, p), ref[at])
                store(elec, p, new)
                if is_even and p == 0 and step == STEPS - 1:
                    send(new)
                if is_even and p == half:
                    for k in range(2):
                        nears[2 * step + k] = new[1 + k]

    pl.when(even)(functools.partial(run, True))
    pl.when(jnp.logical_not(even))(functools.partial(run, False))
    copies[3].wait()
    lay_out(forward, weights)
    copies[4].wait()


def past_near(near, elec):
    return (near[0] + COURANT * elec[Z, 0], near[1] - COURANT * elec[Y, 0])


def lay_out(forward, weights):
    depth, count, ny = forward.shape[1:]
    nz = weights.shape[3]
    blank = jnp.zeros(((nz - depth) // 2, ny), jnp.float32)
    for p in range(count):
        for c in range(6):
            slab = forward[c, :, p, :] * (SENS_SCALE if c < 3 else -SENS_SCALE)
            weights[c, p] = jnp.transpose(jnp.concatenate([blank, slab, blank], 0))


LEFT_MAG = {1: 1, 2: 2, 3: 3, 4: 2, 5: 1}
LEFT_ELEC = {1: 1, 2: 2, 3: 2, 4: 1, 5: 0}
RIGHT_MAG = {1: 0, 2: 1, 3: 2, 4: 1, 5: 0}
RIGHT_ELEC = {1: 1, 2: 2, 3: 2, 4: 1, 5: 0}


def beyond_left(step, elec, side_e, side_m):
    for j in range(LEFT_MAG[step]):
        if j == 0:
            far = (elec[Y, 0], elec[Z, 0])
        else:
            far = (side_e[Y, j - 1], side_e[Z, j - 1])
        store(side_m, j, magnetic_plane(planes(side_e, j), far, planes(side_m, j)))


def beyond_left_electric(step, side_e, side_m, side_eps):
    for j in range(LEFT_ELEC[step]):
        past = (side_m[Y, j + 1], side_m[Z, j + 1])
        store(side_e, j, electric_plane(planes(side_m, j), past, planes(side_e, j), side_eps[j]))


def beyond_right(step, mag, side_e, side_m, side_eps, last):
    for j in range(RIGHT_MAG[step]):
        far = (side_e[Y, j + 1], side_e[Z, j + 1])
        store(side_m, j, magnetic_plane(planes(side_e, j), far, planes(side_m, j)))
    for j in range(RIGHT_ELEC[step]):
        if j == 0:
            past = (mag[Y, last], mag[Z, last])
        else:
            past = (side_m[Y, j - 1], side_m[Z, j - 1])
        store(side_e, j, electric_plane(planes(side_m, j), past, planes(side_e, j), side_eps[j]))


def open_kernel(steps, *refs):
    first, ending = steps[0], steps[-1] == STEPS
    names = ["role", "block", "nears", "opening", "accum_in"]
    names += ["elec_in", "mag_in", "msgs", "side_e_in", "side_m_in"] * (first > 1)
    names += ["late_in", "weights", "ids"] * ending
    names += ["elec_out", "mag_out", "accum_out", "pillars"] * ending
    names += ["elec", "mag", "accum", "side_e", "side_m"]
    names += ["late"] * (first == 1) + ["sems"] * ending
    r = dict(zip(names, refs, strict=True))
    role, block, nears, opening, accum_in = refs[:5]
    elec_in, mag_in, eps = parts(block)
    if first > 1:
        elec_in, mag_in = r["elec_in"], r["mag_in"]
    elec, mag, accum, side_e, side_m = (r[n] for n in ("elec", "mag", "accum", "side_e", "side_m"))
    count = eps.shape[0]
    last = count - 1
    even = role[0] == 0
    side_eps = opening.at[4:6]
    reached = min(first - 1, STEPS + 1 - first)
    for j in range(3):
        for c in range(3):
            if j < reached:
                side_e[c, j] = r["side_e_in"][c, j]
                side_m[c, j] = r["side_m_in"][c, j]
            elif first < STEPS:
                side_e[c, j] = jnp.zeros(eps.shape[1:], jnp.float32)
                side_m[c, j] = jnp.zeros(eps.shape[1:], jnp.float32)

    pending = []

    def put(src, dst):
        copy = pltpu.make_async_copy(src, dst, r["sems"].at[len(pending)])
        copy.start()
        pending.append(copy)

    def run(is_even):
        pending.clear()
        totals = []
        scale = role[1 if is_even else 2].astype(jnp.float32)
        if first == 1:
            far = (opening[0], opening[1])
            if is_even:
                far = past_near(far, elec_in)
            factor = scale
            for p in range(count):
                factor = factor * (COURANT * COURANT * eps[p])
            for k in range(2):
                r["late"][k] = factor * far[k]
        for step in steps:
            src_e, src_m = (elec_in, mag_in) if step == steps[0] else (elec, mag)
            near = (nears[2 * step - 2], nears[2 * step - 1])
            if step == STEPS:
                near = (near[0] + r["late_in"][0], near[1] + r["late_in"][1])
            ref, at = (opening if step < 3 else r["msgs"]), 2 * ((step - 1) % 2)
            far = (ref[at], ref[at + 1])
            if is_even:
                beyond = near
                beyond_left(step, src_e, side_e, side_m)
                past0 = ((far[0] + side_m[Y, 0]) * scale, (far[1] + side_m[Z, 0]) * scale)
            else:
                beyond = ((far[0] + side_e[Y, 0]) * scale, (far[1] + side_e[Z, 0]) * scale)
                past0 = past_near(near, src_e)
            waves = (math.cos(ANGULAR * step), math.sin(ANGULAR * step))
            src_a = accum_in if step == steps[0] else accum

            def magnetic_at(p):
                nxt = (src_e[Y, p + 1], src_e[Z, p + 1]) if p < last else beyond
                store(mag, p, magnetic_plane(planes(src_e, p), nxt, planes(src_m, p)))

            def electric_at(p):
                past = (mag[Y, p - 1], mag[Z, p - 1]) if p else past0
                new = electric_plane(planes(mag, p), past, planes(src_e, p), eps[p])
                store(elec, p, new)
                for c in range(6):
                    accum[c, p] = src_a[c, p] + waves[c // 3] * new[c % 3]

            if step < STEPS:
                for p in range(count):
                    magnetic_at(p)
                if is_even:
                    beyond_left_electric(step, side_e, side_m, side_eps)
                else:
                    beyond_right(step, mag, side_e, side_m, side_eps, last)
                for p in range(count):
                    electric_at(p)
                continue
            for p in range(count):
                magnetic_at(p)
                put(mag.at[:, p], r["mag_out"].at[:, p])
                electric_at(p)
                put(elec.at[:, p], r["elec_out"].at[:, p])
                put(accum.at[:, p], r["accum_out"].at[:, p])
            for p in range(count):
                total = accum[0, p] * r["weights"][0, p]
                for c in range(1, 6):
                    total = total + accum[c, p] * r["weights"][c, p]
                totals.append(total)
        if ending:
            r["pillars"][...] = pillar_terms(totals, r["ids"], r["pillars"].shape[0])
        for copy in pending:
            copy.wait()

    pl.when(even)(functools.partial(run, True))
    pl.when(jnp.logical_not(even))(functools.partial(run, False))


def pillar_terms(totals, ids, owners):
    row = lax.dot_general(
        jnp.ones((8, totals[0].shape[1]), jnp.float32), jnp.concatenate(totals, 0), (((1,), (1,)), ((), ())),
        precision=lax.Precision.HIGHEST, preferred_element_type=jnp.float32,
    )[0:1]
    each = totals[0].shape[0]
    ids = jnp.concatenate([ids[p : p + 1] for p in range(len(totals))], 1)
    owner = lax.broadcasted_iota(jnp.int32, (owners, ids.shape[1]), 0)
    label = lax.broadcasted_iota(jnp.int32, (each, ids.shape[1]), 0)
    high = lax.div(ids, jnp.int32(each))
    return lax.dot_general(
        jnp.where(owner == high, row, 0.0),
        jnp.where(label == ids - each * high, 1.0, 0.0),
        (((1,), (1,)), ((), ())),
        precision=lax.Precision.HIGHEST, preferred_element_type=jnp.float32,
    )


def call(kernel, args, outs, scratch=(), smem=1, fast=(), slow_outs=0, copies=0, slow=()):
    args = [
        pltpu.with_memory_space_constraint(a, pltpu.VMEM if i in fast else pltpu.HBM) if i >= smem else a
        for i, a in enumerate(args)
    ]
    return pl.pallas_call(
        kernel,
        out_shape=[
            shape_of(*o) if i < slow_outs else pltpu.VMEM(o, jnp.float32) for i, o in enumerate(outs)
        ],
        in_specs=[SMEM if i < smem else HBM if i in slow else VMEM for i in range(len(args))],
        out_specs=[HBM] * slow_outs + [VMEM] * (len(outs) - slow_outs),
        scratch_shapes=[pltpu.VMEM(d, jnp.float32) for d in scratch]
        + [pltpu.SemaphoreType.DMA((copies,))] * (copies > 0),
        compiler_params=pltpu.CompilerParams(vmem_limit_bytes=12 * 2**20),
        cost_estimate=pl.CostEstimate(flops=1, bytes_accessed=1, transcendentals=0),
    )(*args)


def shape_of(*dims):
    return jax.ShapeDtypeStruct(dims, jnp.float32)


def summed(sums):
    return jnp.sum(lax.all_to_all(sums, "gx", 0, 0, tiled=True), 0)


def per_device(electric, magnetic, inv_eps, accum, forward, pillar_ids):
    size = lax.axis_size("gx")
    me = lax.axis_index("gx")
    role = jnp.stack([me % 2, jnp.where(me == 0, 0, 1), jnp.where(me == size - 1, 0, 1)]).astype(jnp.int32)
    count, ny, nz = inv_eps.shape
    same_chip = [(i, i ^ 1) for i in range(size)]
    inner = range(1, size - 1, 2)
    next_chip = [(i, i + 1) for i in inner] + [(i + 1, i) for i in inner]

    field, side = electric.shape, (3, 3, ny, nz)

    def to_mate(block):
        return lax.ppermute(block, "gx", same_chip)

    def to_chip(block):
        return lax.ppermute(block, "gx", next_chip)

    opening, middle = call(
        early_kernel,
        [role, electric, magnetic, inv_eps],
        [(6, ny, nz), (4, ny, nz)],
        scratch=[field, field],
    )
    opening = to_chip(opening)
    middle = to_chip(middle)
    mate = [to_mate(electric), to_mate(magnetic), to_mate(inv_eps)]
    block, ending, nears, weights, total = call(
        closed_kernel,
        [role, *mate, electric, magnetic, inv_eps, forward, accum],
        [(7, *inv_eps.shape), (2, ny, nz), (2 * STEPS, ny, nz), accum.shape, accum.shape],
        scratch=[(3, 2 * count, ny, nz)] * 2 + [forward.shape],
        fast=(1, 2, 3),
        slow=range(4, 9),
        copies=5,
    )
    ending = to_chip(ending)
    kept = [field, field, accum.shape, side, side]
    elec, mag, total, *sides, late = call(
        functools.partial(open_kernel, (1, 2)),
        [role, block, nears, opening, total],
        kept + [(2, ny, nz)],
        fast=range(1, 5),
    )
    late = to_mate(late)
    elec, mag, total, *sides = call(
        functools.partial(open_kernel, (3, 4)),
        [role, block, nears, opening, total, elec, mag, middle, *sides],
        kept,
        fast=range(1, 10),
    )
    electric, magnetic, accum, sums = call(
        functools.partial(open_kernel, (5,)),
        [role, block, nears, opening, total, elec, mag, ending, *sides, late, weights, pillar_ids],
        [field, field, accum.shape, (size, ny)],
        scratch=kept,
        fast=range(1, 12),
        slow_outs=3,
        copies=3 * count,
    )
    return electric, magnetic, accum, summed(sums)


def solution(mesh):
    return jax.shard_map(
        per_device,
        mesh=mesh,
        in_specs=(
            P(None, ("design", "gx"), None, None),
            P(None, ("design", "gx"), None, None),
            P(("design", "gx"), None, None),
            P(None, ("design", "gx"), None, None),
            P(None, None, ("design", "gx"), None),
            P("gx", None),
        ),
        out_specs=(
            P(None, ("design", "gx"), None, None),
            P(None, ("design", "gx"), None, None),
            P(None, ("design", "gx"), None, None),
            P(("design", "gx")),
        ),
        check_vma=False,
    )
```

```python
import functools
import math

import jax
import jax.numpy as jnp
from jax import lax
from jax.experimental import pallas as pl
from jax.experimental.pallas import tpu as pltpu
from jax.sharding import PartitionSpec as P

STEPS = 5
COURANT = 0.5
ANGULAR = 0.3
SENS_SCALE = 0.05
X, Y, Z = 0, 1, 2
VMEM = pl.BlockSpec(memory_space=pltpu.VMEM)
SMEM = pl.BlockSpec(memory_space=pltpu.SMEM)
HBM = pl.BlockSpec(memory_space=pltpu.HBM)


def shifted(field, axis, ahead):
    size = field.shape[axis]
    where = lax.broadcasted_iota(jnp.int32, field.shape, axis)
    if ahead:
        return jnp.where(where == size - 1, 0.0, pltpu.roll(field, size - 1, axis))
    return jnp.where(where == 0, 0.0, pltpu.roll(field, 1, axis))


def magnetic_plane(elec, beyond, mag):
    ex, ey, ez = elec
    curl_x = shifted(ez, 0, True) - ez - (shifted(ey, 1, True) - ey)
    far_y, far_z = beyond if beyond is not None else (0.0, 0.0)
    curl_y = shifted(ex, 1, True) - ex - (far_z - ez)
    curl_z = far_y - ey - (shifted(ex, 0, True) - ex)
    return [
        None if m is None else m - COURANT * c
        for m, c in zip(mag, (curl_x, curl_y, curl_z))
    ]


def electric_plane(mag, before, elec, eps):
    hx, hy, hz = mag
    past_y, past_z = before if before is not None else (0.0, 0.0)
    rot_x = hz - shifted(hz, 0, False) - (hy - shifted(hy, 1, False))
    rot_y = hx - shifted(hx, 1, False) - (hz - past_z)
    rot_z = hy - past_y - (hx - shifted(hx, 0, False))
    half = COURANT * eps
    return [e + half * r for e, r in zip(elec, (rot_x, rot_y, rot_z))]


def planes(ref, p):
    return [ref[c, p] for c in range(3)]


def store(ref, p, values):
    for c, v in enumerate(values):
        ref[c, p] = v


def magnetic_all(elec, mag, count, beyond):
    for p in range(count):
        far = (elec[Y, p + 1], elec[Z, p + 1]) if p + 1 < count else beyond
        store(mag, p, magnetic_plane(planes(elec, p), far, planes(mag, p)))


def electric_all(elec, mag, eps, count, before):
    for p in range(count):
        past = (mag[Y, p - 1], mag[Z, p - 1]) if p else before
        store(elec, p, electric_plane(planes(mag, p), past, planes(elec, p), eps[p]))


def needed(wanted_mag, wanted_elec, count):
    mag, elec = dict(wanted_mag), dict(wanted_elec)
    for step in range(STEPS, 0, -1):
        elec[step] = set(elec.get(step, ()))
        mag[step] = set(mag.get(step, ()))
        mag[step] |= elec[step] | {p - 1 for p in elec[step] if p}
        elec[step - 1] = set(elec.get(step - 1, ())) | elec[step] | mag[step]
        elec[step - 1] |= {p + 1 for p in mag[step] if p + 1 < count}
        mag[step - 1] = set(mag.get(step - 1, ())) | mag[step]
    return mag, elec


def parts(block):
    return block.at[0:3], block.at[3:6], block.at[6]


def early_kernel(role, own_e, own_m, own_eps, msg_a, msg_b, elec, mag):
    count = own_e.shape[1]
    last = count - 1
    even = role[0] == 0

    def send(step, value):
        ref = msg_a if step < 3 else msg_b
        for k in range(2):
            ref[2 * ((step - 1) % 2) + k] = value[1 + k]

    def run(is_even):
        if is_even:
            want_m, want_e = {}, {s: {0} for s in range(1, 4)}
        else:
            want_m, want_e = {s: {last} for s in range(1, 5)}, {}
        need_m, need_e = needed(want_m, want_e, count)
        for k in range(2):
            msg_a[4 + k] = own_eps[k if is_even else last - k]
        if is_even:
            send(1, planes(own_e, 0))
        for step in range(1, 5):
            src_e, src_m = (own_e, own_m) if step == 1 else (elec, mag)
            for p in sorted(need_m[step]):
                far = (src_e[Y, p + 1], src_e[Z, p + 1]) if p < last else None
                new = magnetic_plane(planes(src_e, p), far, planes(src_m, p))
                store(mag, p, new)
                if not is_even and p == last:
                    send(step, new)
            for p in sorted(need_e[step]):
                past = (mag[Y, p - 1], mag[Z, p - 1]) if p else None
                new = electric_plane(planes(mag, p), past, planes(src_e, p), own_eps[p])
                store(elec, p, new)
                if is_even and p == 0:
                    send(step + 1, new)

    pl.when(even)(functools.partial(run, True))
    pl.when(jnp.logical_not(even))(functools.partial(run, False))


def closed_kernel(role, mate_e, mate_m, mate_eps, *refs):
    sources, (block, msg, nears, weights, total, elec, mag, forward, sems) = refs[:5], refs[5:]
    own_e, own_m, own_eps = parts(block)
    copies = [
        pltpu.make_async_copy(src, dst, sems.at[i])
        for i, (src, dst) in enumerate(zip(sources, (own_e, own_m, own_eps, forward, total)))
    ]
    for copy in copies:
        copy.start()
    for copy in copies[:3]:
        copy.wait()
    half = own_e.shape[1]
    count = 2 * half
    even = role[0] == 0

    def send(value):
        for k in range(2):
            msg[k] = value[1 + k]

    def run(is_even):
        steps = range(1, STEPS + 1)
        if is_even:
            want_m, want_e = {}, {s: {0, half} if s > 3 else {half} for s in steps if s < STEPS}
        else:
            want_m, want_e = {s: {half - 1, count - 1} if s > 4 else {half - 1} for s in steps}, {}
        need_m, need_e = needed(want_m, want_e, count)

        def first(own, mate, p):
            ref = own if (p < half) == is_even else mate
            return ref, p % half

        def all_of(step, pair, ref, p):
            if step > 1:
                return planes(ref, p)
            return planes(*first(*pair, p))

        def two_of(step, pair, ref, p):
            return tuple(all_of(step, pair, ref, p)[1:])

        pair_e, pair_m = (own_e, mate_e), (own_m, mate_m)
        if is_even:
            for k in range(2):
                nears[k] = mate_e[1 + k, 0]
        for step in steps:
            for p in sorted(need_m[step]):
                far = two_of(step, pair_e, elec, p + 1) if p + 1 < count else None
                here = all_of(step, pair_e, elec, p)
                new = magnetic_plane(here, far, all_of(step, pair_m, mag, p))
                store(mag, p, new)
                if not is_even and p == count - 1 and step == STEPS:
                    send(new)
                if not is_even and p == half - 1:
                    nears[2 * (step - 1)] = new[Y] - COURANT * far[1]
                    nears[2 * (step - 1) + 1] = new[Z] + COURANT * far[0]
            for p in sorted(need_e[step]):
                past = (mag[Y, p - 1], mag[Z, p - 1]) if p else None
                ref, at = first(own_eps, mate_eps, p)
                new = electric_plane(planes(mag, p), past, all_of(step, pair_e, elec, p), ref[at])
                store(elec, p, new)
                if is_even and p == 0 and step == STEPS - 1:
                    send(new)
                if is_even and p == half:
                    for k in range(2):
                        nears[2 * step + k] = new[1 + k]

    pl.when(even)(functools.partial(run, True))
    pl.when(jnp.logical_not(even))(functools.partial(run, False))
    copies[3].wait()
    lay_out(forward, weights)
    copies[4].wait()


def past_near(near, elec):
    return (near[0] + COURANT * elec[Z, 0], near[1] - COURANT * elec[Y, 0])


def lay_out(forward, weights):
    depth, count, ny = forward.shape[1:]
    nz = weights.shape[3]
    blank = jnp.zeros(((nz - depth) // 2, ny), jnp.float32)
    for p in range(count):
        for c in range(6):
            slab = forward[c, :, p, :] * (SENS_SCALE if c < 3 else -SENS_SCALE)
            weights[c, p] = jnp.transpose(jnp.concatenate([blank, slab, blank], 0))


LEFT_MAG = {1: 1, 2: 2, 3: 3, 4: 2, 5: 1}
LEFT_ELEC = {1: 1, 2: 2, 3: 2, 4: 1, 5: 0}
RIGHT_MAG = {1: 0, 2: 1, 3: 2, 4: 1, 5: 0}
RIGHT_ELEC = {1: 1, 2: 2, 3: 2, 4: 1, 5: 0}


def pushed(far):
    return jnp.zeros_like(far[0]), COURANT * far[1], -COURANT * far[0]


def beyond_left(step, elec, side_e, side_m, out_m):
    for j in range(LEFT_MAG[step]):
        if j == 0:
            far = (elec[Y, 0], elec[Z, 0])
        else:
            far = (side_e[Y, j - 1], side_e[Z, j - 1])
        if j == step - 1:
            store(out_m, j, pushed(far))
        else:
            store(out_m, j, magnetic_plane(planes(side_e, j), far, planes(side_m, j)))


def beyond_left_electric(step, side_e, side_m, side_eps, out_e):
    for j in range(LEFT_ELEC[step]):
        past = (side_m[Y, j + 1], side_m[Z, j + 1]) if j + 1 < LEFT_MAG[step] else None
        here = planes(side_m, j)
        blank = jnp.zeros_like(here[0])
        before = [blank] * 3 if j == step - 1 else planes(side_e, j)
        store(out_e, j, electric_plane(here, past, before, side_eps[j]))


def beyond_right(step, mag, side_e, side_m, side_eps, last, out_e, out_m):
    for j in range(RIGHT_MAG[step]):
        far = (side_e[Y, j + 1], side_e[Z, j + 1]) if j + 1 < step - 1 else None
        here = planes(side_e, j)
        before = [jnp.zeros_like(here[0])] * 3 if j == step - 2 else planes(side_m, j)
        store(out_m, j, magnetic_plane(here, far, before))
    for j in range(RIGHT_ELEC[step]):
        if j == 0:
            past = (mag[Y, last], mag[Z, last])
        else:
            past = (out_m[Y, j - 1], out_m[Z, j - 1])
        if j == step - 1:
            x, y, z = pushed(past)
            store(out_e, j, (x, y * side_eps[j], z * side_eps[j]))
        else:
            new = electric_plane(planes(out_m, j), past, planes(side_e, j), side_eps[j])
            store(out_e, j, new)


def open_kernel(steps, *refs):
    first, ending = steps[0], steps[-1] == STEPS
    names = ["role", "block", "nears", "opening", "accum_in"]
    names += ["elec_in", "mag_in", "msgs", "side_e_in", "side_m_in"] * (first > 1)
    names += ["late_in", "weights", "ids"] * ending
    names += ["elec_out", "mag_out", "accum_out", "pillars"] * ending
    names += ["elec", "mag", "accum", "side_e", "side_m"]
    names += ["late"] * (first == 1) + ["sems"] * ending
    r = dict(zip(names, refs, strict=True))
    role, block, nears, opening, accum_in = refs[:5]
    elec_in, mag_in, eps = parts(block)
    if first > 1:
        elec_in, mag_in = r["elec_in"], r["mag_in"]
    elec, mag, accum, side_e, side_m = (r[n] for n in ("elec", "mag", "accum", "side_e", "side_m"))
    count = eps.shape[0]
    last = count - 1
    even = role[0] == 0
    side_eps = opening.at[4:6]
    pending = []

    def put(src, dst):
        copy = pltpu.make_async_copy(src, dst, r["sems"].at[len(pending)])
        copy.start()
        pending.append(copy)

    def run(is_even):
        pending.clear()
        totals = []
        scale = role[1 if is_even else 2].astype(jnp.float32)
        if first == 1:
            far = (opening[0], opening[1])
            if is_even:
                far = past_near(far, elec_in)
            factor = scale
            for p in range(count):
                factor = factor * (COURANT * COURANT * eps[p])
            for k in range(2):
                r["late"][k] = factor * far[k]
        for step in steps:
            src_e, src_m = (elec_in, mag_in) if step == steps[0] else (elec, mag)
            near = (nears[2 * step - 2], nears[2 * step - 1])
            if step == STEPS:
                near = (near[0] + r["late_in"][0], near[1] + r["late_in"][1])
            from_e, from_m = side_e, side_m
            if step == first > 1:
                from_e, from_m = r["side_e_in"], r["side_m_in"]
            ref, at = (opening if step < 3 else r["msgs"]), 2 * ((step - 1) % 2)
            far = (ref[at], ref[at + 1])
            if is_even:
                beyond = near
                beyond_left(step, src_e, from_e, from_m, side_m)
                past0 = ((far[0] + side_m[Y, 0]) * scale, (far[1] + side_m[Z, 0]) * scale)
            else:
                beyond = far
                if step > 1:
                    beyond = (far[0] + from_e[Y, 0], far[1] + from_e[Z, 0])
                beyond = (beyond[0] * scale, beyond[1] * scale)
                past0 = past_near(near, src_e)
            waves = (math.cos(ANGULAR * step), math.sin(ANGULAR * step))
            src_a = accum_in if step == steps[0] else accum

            def magnetic_at(p):
                nxt = (src_e[Y, p + 1], src_e[Z, p + 1]) if p < last else beyond
                store(mag, p, magnetic_plane(planes(src_e, p), nxt, planes(src_m, p)))

            def electric_at(p):
                past = (mag[Y, p - 1], mag[Z, p - 1]) if p else past0
                new = electric_plane(planes(mag, p), past, planes(src_e, p), eps[p])
                store(elec, p, new)
                for c in range(6):
                    accum[c, p] = src_a[c, p] + waves[c // 3] * new[c % 3]

            if step < STEPS:
                for p in range(count):
                    magnetic_at(p)
                if is_even:
                    beyond_left_electric(step, from_e, side_m, side_eps, side_e)
                else:
                    beyond_right(step, mag, from_e, from_m, side_eps, last, side_e, side_m)
                for p in range(count):
                    electric_at(p)
                continue
            for p in range(count):
                magnetic_at(p)
                put(mag.at[:, p], r["mag_out"].at[:, p])
                electric_at(p)
                put(elec.at[:, p], r["elec_out"].at[:, p])
                put(accum.at[:, p], r["accum_out"].at[:, p])
            for p in range(count):
                total = accum[0, p] * r["weights"][0, p]
                for c in range(1, 6):
                    total = total + accum[c, p] * r["weights"][c, p]
                totals.append(total)
        if ending:
            r["pillars"][...] = pillar_terms(totals, r["ids"], r["pillars"].shape[0])
        for copy in pending:
            copy.wait()

    pl.when(even)(functools.partial(run, True))
    pl.when(jnp.logical_not(even))(functools.partial(run, False))


def pillar_terms(totals, ids, owners):
    row = lax.dot_general(
        jnp.ones((8, totals[0].shape[1]), jnp.float32), jnp.concatenate(totals, 0), (((1,), (1,)), ((), ())),
        precision=lax.Precision.HIGHEST, preferred_element_type=jnp.float32,
    )[0:1]
    each = totals[0].shape[0]
    ids = jnp.concatenate([ids[p : p + 1] for p in range(len(totals))], 1)
    owner = lax.broadcasted_iota(jnp.int32, (owners, ids.shape[1]), 0)
    label = lax.broadcasted_iota(jnp.int32, (each, ids.shape[1]), 0)
    high = lax.div(ids, jnp.int32(each))
    return lax.dot_general(
        jnp.where(owner == high, row, 0.0),
        jnp.where(label == ids - each * high, 1.0, 0.0),
        (((1,), (1,)), ((), ())),
        precision=lax.Precision.HIGHEST, preferred_element_type=jnp.float32,
    )


def call(kernel, args, outs, scratch=(), smem=1, fast=(), slow_outs=0, copies=0, slow=()):
    args = [
        pltpu.with_memory_space_constraint(a, pltpu.VMEM if i in fast else pltpu.HBM) if i >= smem else a
        for i, a in enumerate(args)
    ]
    return pl.pallas_call(
        kernel,
        out_shape=[
            shape_of(*o) if i < slow_outs else pltpu.VMEM(o, jnp.float32) for i, o in enumerate(outs)
        ],
        in_specs=[SMEM if i < smem else HBM if i in slow else VMEM for i in range(len(args))],
        out_specs=[HBM] * slow_outs + [VMEM] * (len(outs) - slow_outs),
        scratch_shapes=[pltpu.VMEM(d, jnp.float32) for d in scratch]
        + [pltpu.SemaphoreType.DMA((copies,))] * (copies > 0),
        compiler_params=pltpu.CompilerParams(vmem_limit_bytes=12 * 2**20),
        cost_estimate=pl.CostEstimate(flops=1, bytes_accessed=1, transcendentals=0),
    )(*args)


def shape_of(*dims):
    return jax.ShapeDtypeStruct(dims, jnp.float32)


def summed(sums):
    return jnp.sum(lax.all_to_all(sums, "gx", 0, 0, tiled=True), 0)


def per_device(electric, magnetic, inv_eps, accum, forward, pillar_ids):
    size = lax.axis_size("gx")
    me = lax.axis_index("gx")
    role = jnp.stack([me % 2, jnp.where(me == 0, 0, 1), jnp.where(me == size - 1, 0, 1)]).astype(jnp.int32)
    count, ny, nz = inv_eps.shape
    same_chip = [(i, i ^ 1) for i in range(size)]
    inner = range(1, size - 1, 2)
    next_chip = [(i, i + 1) for i in inner] + [(i + 1, i) for i in inner]

    field, side = electric.shape, (3, 3, ny, nz)

    def to_mate(block):
        return lax.ppermute(block, "gx", same_chip)

    def to_chip(block):
        return lax.ppermute(block, "gx", next_chip)

    opening, middle = call(
        early_kernel,
        [role, electric, magnetic, inv_eps],
        [(6, ny, nz), (4, ny, nz)],
        scratch=[field, field],
    )
    opening = to_chip(opening)
    middle = to_chip(middle)
    mate = [to_mate(electric), to_mate(magnetic), to_mate(inv_eps)]
    block, ending, nears, weights, total = call(
        closed_kernel,
        [role, *mate, electric, magnetic, inv_eps, forward, accum],
        [(7, *inv_eps.shape), (2, ny, nz), (2 * STEPS, ny, nz), accum.shape, accum.shape],
        scratch=[(3, 2 * count, ny, nz)] * 2 + [forward.shape],
        fast=(1, 2, 3),
        slow=range(4, 9),
        copies=5,
    )
    ending = to_chip(ending)
    kept = [field, field, accum.shape, side, side]
    elec, mag, total, *sides, late = call(
        functools.partial(open_kernel, (1, 2)),
        [role, block, nears, opening, total],
        kept + [(2, ny, nz)],
        fast=range(1, 5),
    )
    late = to_mate(late)
    elec, mag, total, *sides = call(
        functools.partial(open_kernel, (3, 4)),
        [role, block, nears, opening, total, elec, mag, middle, *sides],
        kept,
        fast=range(1, 10),
    )
    electric, magnetic, accum, sums = call(
        functools.partial(open_kernel, (5,)),
        [role, block, nears, opening, total, elec, mag, ending, *sides, late, weights, pillar_ids],
        [field, field, accum.shape, (size, ny)],
        scratch=kept,
        fast=range(1, 12),
        slow_outs=3,
        copies=3 * count,
    )
    return electric, magnetic, accum, summed(sums)


def solution(mesh):
    return jax.shard_map(
        per_device,
        mesh=mesh,
        in_specs=(
            P(None, ("design", "gx"), None, None),
            P(None, ("design", "gx"), None, None),
            P(("design", "gx"), None, None),
            P(None, ("design", "gx"), None, None),
            P(None, None, ("design", "gx"), None),
            P("gx", None),
        ),
        out_specs=(
            P(None, ("design", "gx"), None, None),
            P(None, ("design", "gx"), None, None),
            P(None, ("design", "gx"), None, None),
            P(("design", "gx")),
        ),
        check_vma=False,
    )
```

```python
import functools
import math

import jax
import jax.numpy as jnp
from jax import lax
from jax.experimental import pallas as pl
from jax.experimental.pallas import tpu as pltpu
from jax.sharding import PartitionSpec as P

STEPS = 5
COURANT = 0.5
ANGULAR = 0.3
SENS_SCALE = 0.05
X, Y, Z = 0, 1, 2
VMEM = pl.BlockSpec(memory_space=pltpu.VMEM)
SMEM = pl.BlockSpec(memory_space=pltpu.SMEM)
HBM = pl.BlockSpec(memory_space=pltpu.HBM)


def shifted(field, axis, ahead):
    size = field.shape[axis]
    where = lax.broadcasted_iota(jnp.int32, field.shape, axis)
    if ahead:
        return jnp.where(where == size - 1, 0.0, pltpu.roll(field, size - 1, axis))
    return jnp.where(where == 0, 0.0, pltpu.roll(field, 1, axis))


def magnetic_plane(elec, beyond, mag):
    ex, ey, ez = elec
    curl_x = shifted(ez, 0, True) - ez - (shifted(ey, 1, True) - ey)
    far_y, far_z = beyond if beyond is not None else (0.0, 0.0)
    curl_y = shifted(ex, 1, True) - ex - (far_z - ez)
    curl_z = far_y - ey - (shifted(ex, 0, True) - ex)
    return [
        None if m is None else m - COURANT * c
        for m, c in zip(mag, (curl_x, curl_y, curl_z))
    ]


def electric_plane(mag, before, elec, eps):
    hx, hy, hz = mag
    past_y, past_z = before if before is not None else (0.0, 0.0)
    rot_x = hz - shifted(hz, 0, False) - (hy - shifted(hy, 1, False))
    rot_y = hx - shifted(hx, 1, False) - (hz - past_z)
    rot_z = hy - past_y - (hx - shifted(hx, 0, False))
    half = COURANT * eps
    return [e + half * r for e, r in zip(elec, (rot_x, rot_y, rot_z))]


def planes(ref, p):
    return [ref[c, p] for c in range(3)]


def store(ref, p, values):
    for c, v in enumerate(values):
        ref[c, p] = v


def magnetic_all(elec, mag, count, beyond):
    for p in range(count):
        far = (elec[Y, p + 1], elec[Z, p + 1]) if p + 1 < count else beyond
        store(mag, p, magnetic_plane(planes(elec, p), far, planes(mag, p)))


def electric_all(elec, mag, eps, count, before):
    for p in range(count):
        past = (mag[Y, p - 1], mag[Z, p - 1]) if p else before
        store(elec, p, electric_plane(planes(mag, p), past, planes(elec, p), eps[p]))


def needed(wanted_mag, wanted_elec, count):
    mag, elec = dict(wanted_mag), dict(wanted_elec)
    for step in range(STEPS, 0, -1):
        elec[step] = set(elec.get(step, ()))
        mag[step] = set(mag.get(step, ()))
        mag[step] |= elec[step] | {p - 1 for p in elec[step] if p}
        elec[step - 1] = set(elec.get(step - 1, ())) | elec[step] | mag[step]
        elec[step - 1] |= {p + 1 for p in mag[step] if p + 1 < count}
        mag[step - 1] = set(mag.get(step - 1, ())) | mag[step]
    return mag, elec


def parts(block):
    return block.at[0:3], block.at[3:6], block.at[6]


def early_kernel(role, own_e, own_m, own_eps, msg_a, msg_b, elec, mag):
    count = own_e.shape[1]
    last = count - 1
    even = role[0] == 0

    def send(step, value):
        ref = msg_a if step < 3 else msg_b
        for k in range(2):
            ref[2 * ((step - 1) % 2) + k] = value[1 + k]

    def run(is_even):
        if is_even:
            want_m, want_e = {}, {s: {0} for s in range(1, 4)}
        else:
            want_m, want_e = {s: {last} for s in range(1, 5)}, {}
        need_m, need_e = needed(want_m, want_e, count)
        for k in range(2):
            msg_a[4 + k] = own_eps[k if is_even else last - k]
        if is_even:
            send(1, planes(own_e, 0))
        for step in range(1, 5):
            src_e, src_m = (own_e, own_m) if step == 1 else (elec, mag)
            for p in sorted(need_m[step]):
                far = (src_e[Y, p + 1], src_e[Z, p + 1]) if p < last else None
                new = magnetic_plane(planes(src_e, p), far, planes(src_m, p))
                store(mag, p, new)
                if not is_even and p == last:
                    send(step, new)
            for p in sorted(need_e[step]):
                past = (mag[Y, p - 1], mag[Z, p - 1]) if p else None
                new = electric_plane(planes(mag, p), past, planes(src_e, p), own_eps[p])
                store(elec, p, new)
                if is_even and p == 0:
                    send(step + 1, new)

    pl.when(even)(functools.partial(run, True))
    pl.when(jnp.logical_not(even))(functools.partial(run, False))


def closed_kernel(role, mate_e, mate_m, mate_eps, *refs):
    sources, (block, msg, nears, weights, total, elec, mag, forward, sems) = refs[:5], refs[5:]
    own_e, own_m, own_eps = parts(block)
    copies = [
        pltpu.make_async_copy(src, dst, sems.at[i])
        for i, (src, dst) in enumerate(zip(sources, (own_e, own_m, own_eps, forward, total)))
    ]
    for copy in copies:
        copy.start()
    for copy in copies[:3]:
        copy.wait()
    half = own_e.shape[1]
    count = 2 * half
    even = role[0] == 0

    def send(value):
        for k in range(2):
            msg[k] = value[1 + k]

    def run(is_even):
        steps = range(1, STEPS + 1)
        if is_even:
            want_m, want_e = {}, {s: {0, half} if s > 3 else {half} for s in steps if s < STEPS}
        else:
            want_m, want_e = {s: {half - 1, count - 1} if s > 4 else {half - 1} for s in steps}, {}
        need_m, need_e = needed(want_m, want_e, count)

        def first(own, mate, p):
            ref = own if (p < half) == is_even else mate
            return ref, p % half

        def all_of(step, pair, ref, p):
            if step > 1:
                return planes(ref, p)
            return planes(*first(*pair, p))

        def two_of(step, pair, ref, p):
            return tuple(all_of(step, pair, ref, p)[1:])

        pair_e, pair_m = (own_e, mate_e), (own_m, mate_m)
        if is_even:
            for k in range(2):
                nears[k] = mate_e[1 + k, 0]
        for step in steps:
            for p in sorted(need_m[step]):
                far = two_of(step, pair_e, elec, p + 1) if p + 1 < count else None
                here = all_of(step, pair_e, elec, p)
                new = magnetic_plane(here, far, all_of(step, pair_m, mag, p))
                store(mag, p, new)
                if not is_even and p == count - 1 and step == STEPS:
                    send(new)
                if not is_even and p == half - 1:
                    nears[2 * (step - 1)] = new[Y] - COURANT * far[1]
                    nears[2 * (step - 1) + 1] = new[Z] + COURANT * far[0]
            for p in sorted(need_e[step]):
                past = (mag[Y, p - 1], mag[Z, p - 1]) if p else None
                ref, at = first(own_eps, mate_eps, p)
                new = electric_plane(planes(mag, p), past, all_of(step, pair_e, elec, p), ref[at])
                store(elec, p, new)
                if is_even and p == 0 and step == STEPS - 1:
                    send(new)
                if is_even and p == half:
                    for k in range(2):
                        nears[2 * step + k] = new[1 + k]

    pl.when(even)(functools.partial(run, True))
    pl.when(jnp.logical_not(even))(functools.partial(run, False))
    copies[3].wait()
    lay_out(forward, weights)
    copies[4].wait()


def past_near(near, elec):
    return (near[0] + COURANT * elec[Z, 0], near[1] - COURANT * elec[Y, 0])


def lay_out(forward, weights):
    depth, count, ny = forward.shape[1:]
    nz = weights.shape[3]
    blank = jnp.zeros(((nz - depth) // 2, ny), jnp.float32)
    for p in range(count):
        for c in range(6):
            slab = forward[c, :, p, :] * (SENS_SCALE if c < 3 else -SENS_SCALE)
            weights[c, p] = jnp.transpose(jnp.concatenate([blank, slab, blank], 0))


LEFT_MAG = {1: 1, 2: 2, 3: 3, 4: 2, 5: 1}
LEFT_ELEC = {1: 1, 2: 2, 3: 2, 4: 1, 5: 0}
RIGHT_MAG = {1: 0, 2: 1, 3: 2, 4: 1, 5: 0}
RIGHT_ELEC = {1: 1, 2: 2, 3: 2, 4: 1, 5: 0}


def pushed(far):
    return jnp.zeros_like(far[0]), COURANT * far[1], -COURANT * far[0]


def beyond_left(step, elec, side_e, side_m, out_m):
    for j in range(LEFT_MAG[step]):
        if j == 0:
            far = (elec[Y, 0], elec[Z, 0])
        else:
            far = (side_e[Y, j - 1], side_e[Z, j - 1])
        if j == step - 1:
            store(out_m, j, pushed(far))
        else:
            store(out_m, j, magnetic_plane(planes(side_e, j), far, planes(side_m, j)))


def beyond_left_electric(step, side_e, side_m, side_eps, out_e):
    for j in range(LEFT_ELEC[step]):
        past = (side_m[Y, j + 1], side_m[Z, j + 1]) if j + 1 < LEFT_MAG[step] else None
        here = planes(side_m, j)
        blank = jnp.zeros_like(here[0])
        before = [blank] * 3 if j == step - 1 else planes(side_e, j)
        store(out_e, j, electric_plane(here, past, before, side_eps[j]))


def beyond_right(step, mag, side_e, side_m, side_eps, last, out_e, out_m):
    for j in range(RIGHT_MAG[step]):
        far = (side_e[Y, j + 1], side_e[Z, j + 1]) if j + 1 < step - 1 else None
        here = planes(side_e, j)
        before = [jnp.zeros_like(here[0])] * 3 if j == step - 2 else planes(side_m, j)
        store(out_m, j, magnetic_plane(here, far, before))
    for j in range(RIGHT_ELEC[step]):
        if j == 0:
            past = (mag[Y, last], mag[Z, last])
        else:
            past = (out_m[Y, j - 1], out_m[Z, j - 1])
        if j == step - 1:
            x, y, z = pushed(past)
            store(out_e, j, (x, y * side_eps[j], z * side_eps[j]))
        else:
            new = electric_plane(planes(out_m, j), past, planes(side_e, j), side_eps[j])
            store(out_e, j, new)


def open_kernel(steps, *refs):
    first, ending = steps[0], steps[-1] == STEPS
    names = ["role", "block", "nears", "opening", "accum_in"]
    names += ["elec_in", "mag_in", "msgs", "side_e_in", "side_m_in"] * (first > 1)
    names += ["late_in", "weights", "ids"] * ending
    names += ["elec_out", "mag_out", "accum_out", "pillars"] * ending
    names += ["elec", "mag", "accum", "side_e", "side_m"]
    names += ["late"] * (first == 1) + ["sems"] * ending
    r = dict(zip(names, refs, strict=True))
    role, block, nears, opening, accum_in = refs[:5]
    elec_in, mag_in, eps = parts(block)
    if first > 1:
        elec_in, mag_in = r["elec_in"], r["mag_in"]
    elec, mag, accum, side_e, side_m = (r[n] for n in ("elec", "mag", "accum", "side_e", "side_m"))
    count = eps.shape[0]
    last = count - 1
    even = role[0] == 0
    side_eps = opening.at[4:6]
    pending = []

    def put(src, dst):
        copy = pltpu.make_async_copy(src, dst, r["sems"].at[len(pending)])
        copy.start()
        pending.append(copy)

    def run(is_even):
        pending.clear()
        totals = []
        scale = role[1 if is_even else 2].astype(jnp.float32)
        if first == 1:
            far = (opening[0], opening[1])
            if is_even:
                far = past_near(far, elec_in)
            factor = scale
            for p in range(count):
                factor = factor * (COURANT * COURANT * eps[p])
            for k in range(2):
                r["late"][k] = factor * far[k]
        for step in steps:
            src_e, src_m = (elec_in, mag_in) if step == steps[0] else (elec, mag)
            near = (nears[2 * step - 2], nears[2 * step - 1])
            if step == STEPS:
                near = (near[0] + r["late_in"][0], near[1] + r["late_in"][1])
            from_e, from_m = side_e, side_m
            if step == first > 1:
                from_e, from_m = r["side_e_in"], r["side_m_in"]
            ref, at = (opening if step < 3 else r["msgs"]), 2 * ((step - 1) % 2)
            far = (ref[at], ref[at + 1])
            if is_even:
                beyond = near
                beyond_left(step, src_e, from_e, from_m, side_m)
                past0 = ((far[0] + side_m[Y, 0]) * scale, (far[1] + side_m[Z, 0]) * scale)
            else:
                beyond = far
                if step > 1:
                    beyond = (far[0] + from_e[Y, 0], far[1] + from_e[Z, 0])
                beyond = (beyond[0] * scale, beyond[1] * scale)
                past0 = past_near(near, src_e)
            waves = (math.cos(ANGULAR * step), math.sin(ANGULAR * step))
            before = (math.cos(ANGULAR * (step - 1)), math.sin(ANGULAR * (step - 1)))

            def magnetic_at(p):
                nxt = (src_e[Y, p + 1], src_e[Z, p + 1]) if p < last else beyond
                store(mag, p, magnetic_plane(planes(src_e, p), nxt, planes(src_m, p)))

            def electric_at(p):
                past = (mag[Y, p - 1], mag[Z, p - 1]) if p else past0
                held = planes(src_e, p)
                new = electric_plane(planes(mag, p), past, held, eps[p])
                store(elec, p, new)
                if step < steps[-1]:
                    return
                for c in range(6):
                    value = accum_in[c, p] + waves[c // 3] * new[c % 3]
                    if step > first:
                        value = value + before[c // 3] * held[c % 3]
                    accum[c, p] = value

            if step < STEPS:
                for p in range(count):
                    magnetic_at(p)
                if is_even:
                    beyond_left_electric(step, from_e, side_m, side_eps, side_e)
                else:
                    beyond_right(step, mag, from_e, from_m, side_eps, last, side_e, side_m)
                for p in range(count):
                    electric_at(p)
                continue
            for p in range(count):
                magnetic_at(p)
                put(mag.at[:, p], r["mag_out"].at[:, p])
                electric_at(p)
                put(elec.at[:, p], r["elec_out"].at[:, p])
                put(accum.at[:, p], r["accum_out"].at[:, p])
            for p in range(count):
                total = accum[0, p] * r["weights"][0, p]
                for c in range(1, 6):
                    total = total + accum[c, p] * r["weights"][c, p]
                totals.append(total)
        if ending:
            r["pillars"][...] = pillar_terms(totals, r["ids"], r["pillars"].shape[0])
        for copy in pending:
            copy.wait()

    pl.when(even)(functools.partial(run, True))
    pl.when(jnp.logical_not(even))(functools.partial(run, False))


def pillar_terms(totals, ids, owners):
    row = lax.dot_general(
        jnp.ones((8, totals[0].shape[1]), jnp.float32), jnp.concatenate(totals, 0), (((1,), (1,)), ((), ())),
        precision=lax.Precision.HIGHEST, preferred_element_type=jnp.float32,
    )[0:1]
    each = totals[0].shape[0]
    ids = jnp.concatenate([ids[p : p + 1] for p in range(len(totals))], 1)
    owner = lax.broadcasted_iota(jnp.int32, (owners, ids.shape[1]), 0)
    label = lax.broadcasted_iota(jnp.int32, (each, ids.shape[1]), 0)
    high = lax.div(ids, jnp.int32(each))
    return lax.dot_general(
        jnp.where(owner == high, row, 0.0),
        jnp.where(label == ids - each * high, 1.0, 0.0),
        (((1,), (1,)), ((), ())),
        precision=lax.Precision.HIGHEST, preferred_element_type=jnp.float32,
    )


def call(kernel, args, outs, scratch=(), smem=1, fast=(), slow_outs=0, copies=0, slow=()):
    args = [
        pltpu.with_memory_space_constraint(a, pltpu.VMEM if i in fast else pltpu.HBM) if i >= smem else a
        for i, a in enumerate(args)
    ]
    return pl.pallas_call(
        kernel,
        out_shape=[
            shape_of(*o) if i < slow_outs else pltpu.VMEM(o, jnp.float32) for i, o in enumerate(outs)
        ],
        in_specs=[SMEM if i < smem else HBM if i in slow else VMEM for i in range(len(args))],
        out_specs=[HBM] * slow_outs + [VMEM] * (len(outs) - slow_outs),
        scratch_shapes=[pltpu.VMEM(d, jnp.float32) for d in scratch]
        + [pltpu.SemaphoreType.DMA((copies,))] * (copies > 0),
        compiler_params=pltpu.CompilerParams(vmem_limit_bytes=12 * 2**20),
        cost_estimate=pl.CostEstimate(flops=1, bytes_accessed=1, transcendentals=0),
    )(*args)


def shape_of(*dims):
    return jax.ShapeDtypeStruct(dims, jnp.float32)


def summed(sums):
    return jnp.sum(lax.all_to_all(sums, "gx", 0, 0, tiled=True), 0)


def per_device(electric, magnetic, inv_eps, accum, forward, pillar_ids):
    size = lax.axis_size("gx")
    me = lax.axis_index("gx")
    role = jnp.stack([me % 2, jnp.where(me == 0, 0, 1), jnp.where(me == size - 1, 0, 1)]).astype(jnp.int32)
    count, ny, nz = inv_eps.shape
    same_chip = [(i, i ^ 1) for i in range(size)]
    inner = range(1, size - 1, 2)
    next_chip = [(i, i + 1) for i in inner] + [(i + 1, i) for i in inner]

    field, side = electric.shape, (3, 3, ny, nz)

    def to_mate(block):
        return lax.ppermute(block, "gx", same_chip)

    def to_chip(block):
        return lax.ppermute(block, "gx", next_chip)

    opening, middle = call(
        early_kernel,
        [role, electric, magnetic, inv_eps],
        [(6, ny, nz), (4, ny, nz)],
        scratch=[field, field],
    )
    opening = to_chip(opening)
    middle = to_chip(middle)
    mate = [to_mate(electric), to_mate(magnetic), to_mate(inv_eps)]
    block, ending, nears, weights, total = call(
        closed_kernel,
        [role, *mate, electric, magnetic, inv_eps, forward, accum],
        [(7, *inv_eps.shape), (2, ny, nz), (2 * STEPS, ny, nz), accum.shape, accum.shape],
        scratch=[(3, 2 * count, ny, nz)] * 2 + [forward.shape],
        fast=(1, 2, 3),
        slow=range(4, 9),
        copies=5,
    )
    ending = to_chip(ending)
    kept = [field, field, accum.shape, side, side]
    elec, mag, total, *sides, late = call(
        functools.partial(open_kernel, (1, 2)),
        [role, block, nears, opening, total],
        kept + [(2, ny, nz)],
        fast=range(1, 5),
    )
    late = to_mate(late)
    elec, mag, total, *sides = call(
        functools.partial(open_kernel, (3, 4)),
        [role, block, nears, opening, total, elec, mag, middle, *sides],
        kept,
        fast=range(1, 10),
    )
    electric, magnetic, accum, sums = call(
        functools.partial(open_kernel, (5,)),
        [role, block, nears, opening, total, elec, mag, ending, *sides, late, weights, pillar_ids],
        [field, field, accum.shape, (size, ny)],
        scratch=kept,
        fast=range(1, 12),
        slow_outs=3,
        copies=3 * count,
    )
    return electric, magnetic, accum, summed(sums)


def solution(mesh):
    return jax.shard_map(
        per_device,
        mesh=mesh,
        in_specs=(
            P(None, ("design", "gx"), None, None),
            P(None, ("design", "gx"), None, None),
            P(("design", "gx"), None, None),
            P(None, ("design", "gx"), None, None),
            P(None, None, ("design", "gx"), None),
            P("gx", None),
        ),
        out_specs=(
            P(None, ("design", "gx"), None, None),
            P(None, ("design", "gx"), None, None),
            P(None, ("design", "gx"), None, None),
            P(("design", "gx")),
        ),
        check_vma=False,
    )
```
